1024 devices in a mesh: grp: 16 (over z, core), dev: 64 (over x, y).
Axes of the slice: x: 8, y: 8, z: 8, core: 2. Of those that a mesh axis runs over, the one named last changes fastest.
Arguments:
- offsets: float32 [3, 1048576], P(None, ('grp', 'dev')), may hold values from -0.5 to 0.5
- strengths: float32 [3, 1048576], P(None, ('grp', 'dev')), may hold values from -6 to 6
- cores: float32 [1048576], P(('grp', 'dev')), may hold values from 0.3 to 0.8
- place: int32 [2, 1048576], P(None, ('grp', 'dev')), may hold values from 0 to 16383, as said below
- near_list: int32 [14, 16384], P(None, ('grp', 'dev')), may hold values from -1 to 16383, as said below
- far_list: int32 [189, 16384], P(None, ('grp', 'dev')), may hold values from 0 to 16383, as said below
Outputs:
- velocity: float32 [3, 2097152], P(None, ('grp', 'dev'))
The draws below stay inside these ranges and needn't reach their ends.
Inputs may be any that keep to these rules, and one draw needn't show every extreme that they name: `place`: row 0 names a cell of the particle's own group (cells of group g are g * 64 * 16 up to 64 * 16 more), row 1 a slot. Each pair of cell and slot is named at most once; a cell's slots are filled from 0 up without gaps, some cell of every device full; the cells of every device are named by exactly 1024 rows; at most 32 rows of one device name cells of one device, and every device has rows that reach that bound. `near_list`: used entries come first and are followed by -1; a cell's used entries differ and name cells of the same group held by the same device, the device before it or the device after it along dev. `far_list`: the entries of index under 189 // 2 name cells of the target cell's group.
All inputs are finite; a program needn't handle non-finite values.
Results may differ from the reference program's by a relative error of at most 0.0003.
Values sent between devices are 32-bit elements; how exact they have to be, the bound alone decides.
A program may use at most 64 MiB of HBM per device.

```python
import math
import jax
import jax.numpy as jnp
from jax import lax

SLOTS = 128
ROWS_DEV = 1024
NEAR = 14
FAR = 189
CELLS_DEV = 16
CAP = 32
CELLS_TOTAL = 16384
ROWS_TOTAL = 1048576
N_GRP = 16
N_DEV = 64


def draw_place(key, part):
    group_n = N_GRP
    device_n = N_DEV
    row_n = ROWS_DEV
    key_perm = jax.random.fold_in(key, 11)
    key_counts = jax.random.fold_in(key, 12)
    key_order = jax.random.fold_in(key, 13)
    key_shuffle = jax.random.fold_in(key, 14)
    dev_range = jnp.arange(device_n, dtype=jnp.int32)
    shift_perm = jnp.argsort(jax.random.randint(key_perm, (group_n, device_n), 0, 1 << 16) * device_n + dev_range[None, :], axis=1).astype(jnp.int32)
    profile = jnp.where(dev_range < 3 * device_n // 8, CAP, jnp.where(dev_range < 5 * device_n // 8, CAP // 2, 0)).astype(jnp.int32)
    cum_incl = jnp.cumsum(profile)
    cum_excl = cum_incl - profile
    row_range = jnp.arange(row_n, dtype=jnp.int32)
    offset_of_row = jnp.sum((cum_incl[None, :] <= row_range[:, None]).astype(jnp.int32), axis=1)
    bucket_pos = row_range - cum_excl[offset_of_row]
    dest_dev = (offset_of_row[None, None, :] + shift_perm[:, :, None]) % device_n
    load_matrix = profile[(dev_range[None, None, :] - shift_perm[:, :, None]) % device_n]
    prior_load = jnp.cumsum(load_matrix, axis=1) - load_matrix
    arrival = jnp.take_along_axis(prior_load, dest_dev, axis=2) + bucket_pos[None, None, :]
    pair_n = CELLS_DEV // 2
    variant = jax.random.randint(key_counts, (group_n, device_n, pair_n), 0, 5)
    variant = variant.at[:, :, 0].set(0)
    first_count = SLOTS - variant * (SLOTS // 8)
    counts = jnp.concatenate([first_count, SLOTS - first_count], axis=2)
    cell_range = jnp.arange(CELLS_DEV, dtype=jnp.int32)
    cell_order = jnp.argsort(jax.random.randint(key_order, (group_n, device_n, CELLS_DEV), 0, 1 << 16) * CELLS_DEV + cell_range, axis=2)
    counts = jnp.take_along_axis(counts, cell_order, axis=2).astype(jnp.int32)
    count_incl = jnp.cumsum(counts, axis=2)
    count_excl = count_incl - counts
    group_range = jnp.arange(group_n, dtype=jnp.int32)[:, None, None]
    sel_incl = count_incl[group_range, dest_dev]
    sel_excl = count_excl[group_range, dest_dev]
    local_cell = jnp.sum((sel_incl <= arrival[..., None]).astype(jnp.int32), axis=3)
    slot_number = arrival - jnp.take_along_axis(sel_excl, local_cell[..., None], axis=3)[..., 0]
    global_cell = (group_range * device_n + dest_dev) * CELLS_DEV + local_cell
    shuffle = jnp.argsort(jax.random.randint(key_shuffle, (group_n, device_n, row_n), 0, 1 << 16) * row_n + row_range, axis=2)
    global_cell = jnp.take_along_axis(global_cell, shuffle, axis=2)
    slot_number = jnp.take_along_axis(slot_number, shuffle, axis=2)
    return jnp.stack([global_cell.reshape(-1), slot_number.reshape(-1)]).astype(jnp.int32)


def draw_near_list(key, part):
    key_score = jax.random.fold_in(key, 21)
    key_level = jax.random.fold_in(key, 22)
    key_count = jax.random.fold_in(key, 23)
    cell_ids = jnp.arange(CELLS_TOTAL, dtype=jnp.int32)
    device_in_group = cell_ids // CELLS_DEV % N_DEV
    window_size = 3 * CELLS_DEV
    window = jnp.arange(window_size, dtype=jnp.int32)
    candidate = (cell_ids // CELLS_DEV)[:, None] * CELLS_DEV - CELLS_DEV + window[None, :]
    invalid = (window[None, :] < CELLS_DEV) & (device_in_group[:, None] == 0) | (window[None, :] >= 2 * CELLS_DEV) & (device_in_group[:, None] == N_DEV - 1)
    scores = jax.random.randint(key_score, (CELLS_TOTAL, window_size), 0, 1 << 16) * window_size + window[None, :] + invalid.astype(jnp.int32) * (1 << 28)
    chosen_order = jnp.argsort(scores, axis=1)[:, :NEAR]
    chosen = jnp.take_along_axis(candidate, chosen_order, axis=1)
    level_dev = jax.random.randint(key_level, (CELLS_TOTAL // CELLS_DEV,), 1, 4)
    level_cells = jnp.repeat(level_dev, CELLS_DEV)
    count_cells = jnp.minimum(NEAR, jax.random.randint(key_count, (CELLS_TOTAL,), 1, NEAR // 3 + 1) * level_cells)
    keep_entry = jnp.arange(NEAR, dtype=jnp.int32)[None, :] < count_cells[:, None]
    return jnp.where(keep_entry, chosen, -1).T.astype(jnp.int32)


def draw_far_list(key, part):
    key_inner = jax.random.fold_in(key, 31)
    key_any = jax.random.fold_in(key, 32)
    cell_ids = jnp.arange(CELLS_TOTAL, dtype=jnp.int32)
    group_size = N_DEV * CELLS_DEV
    group_start = cell_ids // group_size * group_size
    inner_ids = jax.random.randint(key_inner, (FAR, CELLS_TOTAL), 0, group_size) + group_start[None, :]
    any_ids = jax.random.randint(key_any, (FAR, CELLS_TOTAL), 0, CELLS_TOTAL)
    first_half = jnp.arange(FAR, dtype=jnp.int32)[:, None] < FAR // 2
    return jnp.where(first_half, inner_ids, any_ids).astype(jnp.int32)


def block_scale(rng, dims, split, least, high):
    factor_of, own = 1.0, jax.random.fold_in(rng, 6)
    for position, shards_of in split:
        draws = jnp.exp(jax.random.uniform(jax.random.fold_in(own, position), (shards_of,), jnp.float32, least / len(split), high / len(split)))
        factor_of = factor_of * jnp.repeat(draws, dims[position] // shards_of).reshape([-1 if axis == position else 1 for axis in range(len(dims))])
    return factor_of


def gaussian(own_key, dims, width, reach, pieces=(), held_as=jnp.bfloat16):
    drawn = jax.random.normal(own_key, dims, jnp.float32) * width
    if len(pieces) > 0:
        drawn = block_scale(own_key, dims, pieces, -0.22, 0.18) * drawn
    return jnp.clip(drawn, min=-reach, max=reach).astype(held_as)


def setup_inputs(seed: int = 0) -> dict:
    seeds = jax.random.split(jax.random.key(seed), 7)
    offsets = jnp.clip(jax.random.uniform(seeds[0], (3, ROWS_TOTAL), jnp.float32, -0.5, 0.5) * block_scale(seeds[0], (3, ROWS_TOTAL), ((1, 1024),), -0.4, 0.0), -0.5, 0.5)
    strengths = gaussian(seeds[1], (3, ROWS_TOTAL), 1.0, 6.0, ((1, 1024),), jnp.float32)
    cores = jnp.clip(jnp.exp(math.log(0.8) - 0.98082923 * jax.random.uniform(seeds[2], (ROWS_TOTAL,), jnp.float32) ** block_scale(seeds[2], (ROWS_TOTAL,), ((0, 1024),), -0.2, 0.2)), 0.3, 0.8)
    place = draw_place(jax.random.fold_in(seeds[6], 71), 0)
    near_list = draw_near_list(jax.random.fold_in(seeds[6], 71), 0)
    far_list = draw_far_list(jax.random.fold_in(seeds[6], 71), 0)
    return {"offsets": offsets, "strengths": strengths, "cores": cores, "place": place, "near_list": near_list, "far_list": far_list}


INV_FOUR_PI = 0.25 / math.pi

def centres(cell_ids):
    coordinate_list = []
    for axis_number in range(3):
        coordinate = jnp.zeros(cell_ids.shape, jnp.int32)
        for bit_level in range(10):
            power_shift = 3 * bit_level + axis_number
            coordinate = coordinate + cell_ids // (1 << power_shift) % 2 * (1 << bit_level)
        coordinate_list.append(coordinate.astype(jnp.float32) + 0.5)
    return jnp.stack(coordinate_list)

def near_terms(target, target_core, source, source_strength, source_core):
    delta_x = target[0][:, :, None] - source[0][:, None, :]
    delta_y = target[1][:, :, None] - source[1][:, None, :]
    delta_z = target[2][:, :, None] - source[2][:, None, :]
    spread = 0.5 * (target_core[:, :, None] ** 2 + source_core[:, None, :] ** 2)
    dist_sq = delta_x * delta_x + delta_y * delta_y + delta_z * delta_z + spread
    weight = INV_FOUR_PI / (dist_sq * jnp.sqrt(dist_sq))
    str_x = source_strength[0][:, None, :]
    str_y = source_strength[1][:, None, :]
    str_z = source_strength[2][:, None, :]
    vel_x = lax.optimization_barrier(jnp.sum(weight * (str_y * delta_z - str_z * delta_y), axis=-1))
    vel_y = lax.optimization_barrier(jnp.sum(weight * (str_z * delta_x - str_x * delta_z), axis=-1))
    vel_z = lax.optimization_barrier(jnp.sum(weight * (str_x * delta_y - str_y * delta_x), axis=-1))
    return jnp.stack([vel_x, vel_y, vel_z])

def far_terms(target, target_core, centre_src, strength_src):
    delta_x = target[0][None] - centre_src[0][:, :, None]
    delta_y = target[1][None] - centre_src[1][:, :, None]
    delta_z = target[2][None] - centre_src[2][:, :, None]
    dist_sq = delta_x * delta_x + delta_y * delta_y + delta_z * delta_z + target_core[None] ** 2
    weight = INV_FOUR_PI / (dist_sq * jnp.sqrt(dist_sq))
    str_x = strength_src[0][:, :, None]
    str_y = strength_src[1][:, :, None]
    str_z = strength_src[2][:, :, None]
    vel_x = lax.optimization_barrier(jnp.sum(weight * (str_y * delta_z - str_z * delta_y), axis=0))
    vel_y = lax.optimization_barrier(jnp.sum(weight * (str_z * delta_x - str_x * delta_z), axis=0))
    vel_z = lax.optimization_barrier(jnp.sum(weight * (str_x * delta_y - str_y * delta_x), axis=0))
    return jnp.stack([vel_x, vel_y, vel_z])

def reference(offsets, strengths, cores, place, near_list, far_list):
    total_slots = CELLS_TOTAL * SLOTS
    slot_index = place[0] * SLOTS + place[1]
    fill_mask = jnp.zeros((total_slots,), jnp.float32).at[slot_index].set(1.0)
    offset_tile = jnp.zeros((3, total_slots), jnp.float32).at[:, slot_index].set(offsets)
    strength_tile = jnp.zeros((3, total_slots), jnp.float32).at[:, slot_index].set(strengths)
    core_tile = jnp.ones((total_slots,), jnp.float32).at[slot_index].set(cores)
    centre_all = centres(jnp.arange(CELLS_TOTAL, dtype=jnp.int32))
    positions = offset_tile.reshape(3, CELLS_TOTAL, SLOTS) + centre_all[:, :, None]
    strength_cells = strength_tile.reshape(3, CELLS_TOTAL, SLOTS)
    core_cells = core_tile.reshape(CELLS_TOTAL, SLOTS)
    fill_cells = fill_mask.reshape(CELLS_TOTAL, SLOTS)
    cell_strength = lax.optimization_barrier(jnp.sum(strength_cells, axis=2))
    block_count = CELLS_TOTAL // CELLS_DEV
    far_blocks = FAR // 27

    def evaluate(points):

        def one_block(block_id):
            first_cell = block_id * CELLS_DEV
            target = lax.dynamic_slice_in_dim(points, first_cell, CELLS_DEV, 1)
            target_core = lax.dynamic_slice_in_dim(core_cells, first_cell, CELLS_DEV, 0)
            near_block = lax.dynamic_slice_in_dim(near_list, first_cell, CELLS_DEV, 1)
            far_block = lax.dynamic_slice_in_dim(far_list, first_cell, CELLS_DEV, 1)

            def near_step(running_sum, entry_ids):
                entry_used = (entry_ids >= 0).astype(jnp.float32)
                source_ids = jnp.maximum(entry_ids, 0)
                term = near_terms(target, target_core, points[:, source_ids], strength_cells[:, source_ids], core_cells[source_ids])
                return (running_sum + entry_used[None, :, None] * term, None)
            near_total, _ = lax.scan(near_step, jnp.zeros((3, CELLS_DEV, SLOTS), jnp.float32), near_block)
            far_ids = far_block.reshape(far_blocks, 27, CELLS_DEV)

            def far_step(running_sum, block_ids):
                term = far_terms(target, target_core, centres(block_ids), cell_strength[:, block_ids])
                return (running_sum + term, None)
            far_total, _ = lax.scan(far_step, jnp.zeros((3, CELLS_DEV, SLOTS), jnp.float32), far_ids)
            return near_total + far_total
        result = lax.map(one_block, jnp.arange(block_count, dtype=jnp.int32))
        return jnp.transpose(result, (1, 0, 2, 3)).reshape(3, CELLS_TOTAL, SLOTS)
    first_pass = evaluate(positions) * fill_cells[None]
    moved = positions + 0.25 * first_pass
    second_pass = evaluate(moved) * fill_cells[None]
    return (0.5 * (first_pass + second_pass)).reshape(3, total_slots)
```

```python
import functools
import math

import jax
import jax.numpy as jnp
from jax import lax
from jax.experimental import pallas as pl
from jax.experimental.pallas import tpu as pltpu
from jax.sharding import PartitionSpec as P

SLOTS = 128
CELLS = 16
CAP = 32
NEAR = 14
FAR = 189
N = 8
INV_FOUR_PI = 0.25 / math.pi
MESH = pl.DeviceIdType.MESH
F32 = jnp.float32
BF16 = jnp.bfloat16

NEAR_CHUNKS = 3 * CELLS
DUMMY = NEAR_CHUNKS
FAR_BASE = NEAR_CHUNKS + 2
CHUNKS = FAR_BASE + 2 * CELLS
FEATS = 48


def nt(a, b):
    return lax.dot_general(a, b, (((1,), (1,)), ((), ())), preferred_element_type=F32)


def nn(a, b):
    return lax.dot_general(a, b, (((1,), (0,)), ((), ())), preferred_element_type=F32)


def rows_of(shape):
    return lax.broadcasted_iota(jnp.int32, shape, len(shape) - 2)


def lanes_of(shape):
    return lax.broadcasted_iota(jnp.int32, shape, len(shape) - 1)


def split2(value):
    high = value.astype(BF16).astype(F32)
    return jnp.concatenate([high, value - high], axis=0)


def route_kernel(
    off_ref, str_ref, core_ref, place_ref, ext_ref, table_ref,
    fields, spread, send1, recv1, send2, recv2, sums, sums_y, sums_x,
    sx_s, sx_r, sy_s, sy_r, halo_s, halo_r, cy_s, cy_r, cx_s, cx_r, cz_s, cz_r, cc_s, cc_r,
):
    dev = lax.axis_index("dev")
    grp = lax.axis_index("grp")
    x, y = dev // N, dev % N
    z, core = grp // 2, grp % 2

    def x_peer(k):
        return (x + k) % N

    def y_peer(k):
        return (y + k) % N

    def z_peer(k):
        return (z + k) % N

    right, left = (dev + 1) % (N * N), (dev + N * N - 1) % (N * N)
    barrier = pltpu.get_barrier_semaphore()
    for k in range(1, N):
        pl.semaphore_signal(barrier, 1, device_id={"dev": x_peer(k) * N + y}, device_id_type=MESH)
        pl.semaphore_signal(barrier, 1, device_id={"dev": x * N + y_peer(k)}, device_id_type=MESH)
        pl.semaphore_signal(barrier, 1, device_id={"grp": z_peer(k) * 2 + core}, device_id_type=MESH)
    pl.semaphore_signal(barrier, 1, device_id={"dev": right}, device_id_type=MESH)
    pl.semaphore_signal(barrier, 1, device_id={"dev": left}, device_id_type=MESH)
    pl.semaphore_signal(barrier, 1, device_id={"grp": z * 2 + (1 - core)}, device_id_type=MESH)

    rows = off_ref.shape[1]
    cell_row = place_ref[0:1, :]
    spot = (cell_row & (CELLS - 1)) * SLOTS + place_ref[1:2, :] + 1
    owner = (cell_row >> 4) & (N * N - 1)
    fields[0:3, :] = off_ref[...]
    fields[3:4, :] = core_ref[...]
    fields[4:5, :] = spot.astype(F32)
    fields[5:8, :] = str_ref[...]
    both = split2(fields[...])
    earlier = rows_of((SLOTS, 2 * SLOTS)) < lanes_of((SLOTS, 2 * SLOTS))
    counter = jnp.where(earlier | (lanes_of((SLOTS, 2 * SLOTS)) >= SLOTS), 1.0, 0.0).astype(BF16)
    carry = jnp.zeros((N * N, SLOTS), F32)
    ranks = []
    for b in range(rows // SLOTS):
        hot = jnp.where(rows_of((N * N, SLOTS)) == owner[:, b * SLOTS : (b + 1) * SLOTS], 1.0, 0.0)
        count = nn(hot.astype(BF16), counter)
        ranks.append(jnp.sum(hot * (count[:, :SLOTS] + carry), axis=0, keepdims=True))
        carry = carry + count[:, SLOTS:]
    rank = jnp.concatenate(ranks, axis=1).astype(jnp.int32)
    low = (owner & 3) * CAP + rank
    high = owner >> 2
    low_hot = jnp.where(rows_of((SLOTS, rows)) == low, 1.0, 0.0).astype(BF16)
    for t in range(2 * N):
        spread[16 * t : 16 * t + 16, 0:rows] = jnp.where(high == t, both, 0.0).astype(BF16)
    packed = nt(spread[:, 0:rows], low_hot)
    for t in range(2 * N):
        send1[t] = packed[16 * t : 16 * t + 8] + packed[16 * t + 8 : 16 * t + 16]

    pl.semaphore_wait(barrier, 3 * (N - 1) + 3)

    copies = []
    for k in range(1, N):
        to = x_peer(k)
        copy = pltpu.make_async_remote_copy(
            src_ref=send1.at[pl.ds(2 * to, 2)], dst_ref=recv1.at[x],
            send_sem=sx_s.at[k], recv_sem=sx_r.at[k],
            device_id={"dev": to * N + y}, device_id_type=MESH,
        )
        copy.start()
        copies.append(copy)
    recv1[x] = send1[pl.ds(2 * x, 2)]
    for copy in copies:
        copy.wait_recv()
    lane_group = lanes_of((8, SLOTS)) // CAP
    for t in range(N):
        for k in range(2):
            tile = None
            for g in range(4):
                part = recv1[4 * k + g, t // 4]
                turn = (g - t % 4) % 4 * CAP
                if turn:
                    part = pltpu.roll(part, turn, 1)
                tile = part if tile is None else jnp.where(lane_group == g, part, tile)
            send2[t, k] = tile
    for k in range(1, N):
        to = y_peer(k)
        copy = pltpu.make_async_remote_copy(
            src_ref=send2.at[to], dst_ref=recv2.at[y],
            send_sem=sy_s.at[k], recv_sem=sy_r.at[k],
            device_id={"dev": x * N + to}, device_id_type=MESH,
        )
        copy.start()
        copies.append(copy)
    recv2[y] = send2[y]
    for copy in copies[N - 1 :]:
        copy.wait_recv()

    slot_rows, sums_rows, both_all = [], [], []
    for t in range(2 * N):
        tile = recv2[t // 2, t % 2]
        spot_row = tile[4:5, :] - 1.0
        cell = jnp.floor(spot_row * (1.0 / SLOTS))
        slot = (spot_row - cell * SLOTS).astype(jnp.int32)
        cell = cell.astype(jnp.int32)
        two = split2(tile)
        both_all.append(two.astype(BF16))
        slot_rows.append(jnp.where(rows_of((SLOTS, SLOTS)) == slot, 1.0, 0.0).astype(BF16))
        sums_rows.append(
            jnp.where(rows_of((SLOTS, SLOTS)) == cell + y * CELLS, 1.0, 0.0).astype(BF16)
        )
        for c in range(CELLS):
            spread[16 * c : 16 * c + 16, t * SLOTS : (t + 1) * SLOTS] = jnp.where(
                cell == c, two, 0.0
            ).astype(BF16)
    cell_sums = nt(jnp.concatenate(both_all, axis=1), jnp.concatenate(sums_rows, axis=1))
    sums[...] = cell_sums[0:8] + cell_sums[8:16]
    sum_copies = []
    for k in range(1, N):
        copy = pltpu.make_async_remote_copy(
            src_ref=sums, dst_ref=sums_y.at[y],
            send_sem=cy_s.at[k], recv_sem=cy_r.at[k],
            device_id={"dev": x * N + y_peer(k)}, device_id_type=MESH,
        )
        copy.start()
        sum_copies.append(copy)
    placed = nt(spread[...], jnp.concatenate(slot_rows, axis=1))
    for c in range(CELLS):
        tile = placed[16 * c : 16 * c + 8] + placed[16 * c + 8 : 16 * c + 16]
        empty = (rows_of((8, SLOTS)) == 3) & (tile[4:5, :] == 0.0)
        ext_ref[CELLS + c] = jnp.where(empty, 1.0, tile)

    halo = []
    for i, (to, at) in enumerate(((right, 0), (left, 2 * CELLS))):
        copy = pltpu.make_async_remote_copy(
            src_ref=ext_ref.at[pl.ds(CELLS, CELLS)], dst_ref=ext_ref.at[pl.ds(at, CELLS)],
            send_sem=halo_s.at[i], recv_sem=halo_r.at[i],
            device_id={"dev": to}, device_id_type=MESH,
        )
        copy.start()
        halo.append(copy)

    total = sums[...]
    for copy in sum_copies:
        copy.wait_recv()
    for k in range(1, N):
        total = total + sums_y[y_peer(k)]
    sums_x[x] = total
    x_copies = []
    for k in range(1, N):
        copy = pltpu.make_async_remote_copy(
            src_ref=sums_x.at[x], dst_ref=sums_x.at[x],
            send_sem=cx_s.at[k], recv_sem=cx_r.at[k],
            device_id={"dev": x_peer(k) * N + y}, device_id_type=MESH,
        )
        copy.start()
        x_copies.append(copy)
    for copy in x_copies:
        copy.wait_recv()
    for comp in range(3):
        table_ref[core, z, comp] = sums_x[:, 5 + comp, :]
    z_copies = []
    for k in range(1, N):
        copy = pltpu.make_async_remote_copy(
            src_ref=table_ref.at[core, z], dst_ref=table_ref.at[core, z],
            send_sem=cz_s.at[k], recv_sem=cz_r.at[k],
            device_id={"grp": z_peer(k) * 2 + core}, device_id_type=MESH,
        )
        copy.start()
        z_copies.append(copy)
    core_copies = []
    for k in range(N):
        if k:
            z_copies[k - 1].wait_recv()
        source = (z + N - k) % N
        copy = pltpu.make_async_remote_copy(
            src_ref=table_ref.at[core, source], dst_ref=table_ref.at[core, source],
            send_sem=cc_s.at[k], recv_sem=cc_r.at[k],
            device_id={"grp": z * 2 + (1 - core)}, device_id_type=MESH,
        )
        copy.start()
        core_copies.append(copy)
    for copy in core_copies + halo:
        copy.wait_recv()
    for copy in copies + sum_copies + x_copies + z_copies + core_copies + halo:
        copy.wait_send()


def halo_kernel(moved_ref, ext_ref, send_sem, recv_sem):
    dev = lax.axis_index("dev")
    right, left = (dev + 1) % (N * N), (dev + N * N - 1) % (N * N)
    barrier = pltpu.get_barrier_semaphore()
    for to in (right, left):
        pl.semaphore_signal(barrier, 1, device_id={"dev": to}, device_id_type=MESH)
    pl.semaphore_wait(barrier, 2)
    halo = []
    for i, to in enumerate((right, left)):
        copy = pltpu.make_async_remote_copy(
            src_ref=moved_ref, dst_ref=ext_ref.at[i],
            send_sem=send_sem.at[i], recv_sem=recv_sem.at[i],
            device_id={"dev": to}, device_id_type=MESH,
        )
        copy.start()
        halo.append(copy)
    for copy in halo:
        copy.wait()


def axis_bits(ids):
    shifted = ids >> jnp.minimum(rows_of(ids.shape), 2)
    value = shifted & 1
    for bit in range(1, 5):
        value = value + ((shifted >> (3 * bit)) & 1) * (1 << bit)
    return value


def source_rows(points, half, flag):
    row = rows_of(points.shape)
    at = jnp.where(row < 3, points, 0.0)
    norm = jnp.sum(at * at, axis=0, keepdims=True) + half
    return jnp.where(row == 3, norm, jnp.where(row == 4, 1.0, jnp.where(row == 5, flag, at)))


def split3(tile):
    high = tile.astype(BF16).astype(F32)
    rest = tile - high
    mid = rest.astype(BF16).astype(F32)
    return high, mid, rest - mid


def moments(points, strength):
    sx, sy, sz = (INV_FOUR_PI * s for s in strength)
    px, py, pz = points
    row = rows_of((8, sx.shape[1]))
    tile = jnp.zeros((8, sx.shape[1]), F32)
    values = (sx, sy, sz, sy * pz - sz * py, sz * px - sx * pz, sx * py - sy * px)
    for r, value in enumerate(values):
        tile = jnp.where(row == r, value, tile)
    return split2(tile).astype(BF16)


def pass_kernel(
    second, near_ref, own_ref, ext_ref, *rest
):
    if second:
        move_ref, moved_ref, first_ref, far_in, out_ref, feat, weight, targ, count, acc = rest
    else:
        table_ref, far_ref, first_ref, moved_ref, far_out, feat, weight, targ, count, acc = rest
    base_id = own_ref[0]
    base = axis_bits(jnp.full((8, SLOTS), base_id, jnp.int32))

    def put(chunk, tile, points):
        high, mid, low = split3(tile)
        feat[chunk] = jnp.concatenate([high, high, mid, mid, high, low], axis=0).astype(BF16)

    def own_tile(l):
        tile = ext_ref[l]
        ids = jnp.full((8, SLOTS), base_id - CELLS + l, jnp.int32)
        centre = (axis_bits(ids) - base).astype(F32)
        return tile, centre

    def near_prep(l, _):
        tile, centre = own_tile(l)
        at = tile
        if second:
            side = l // CELLS
            within = l - side * CELLS
            at = jnp.where(
                side == 1, moved_ref[within],
                jnp.where(side == 0, move_ref[0, within], move_ref[1, within]),
            )
        points = at + centre
        core = tile[3:4, :]
        half = 0.5 * core * core
        put(l, source_rows(points, half, 0.0), points)
        weight[l] = moments(
            (points[0:1], points[1:2], points[2:3]), (tile[5:6], tile[6:7], tile[7:8])
        )
        return 0

    lax.fori_loop(0, NEAR_CHUNKS, near_prep, 0)
    feat[DUMMY] = jnp.zeros((FEATS, SLOTS), BF16)
    weight[DUMMY] = jnp.zeros((16, SLOTS), BF16)

    def target_prep(c, _):
        tile, centre = own_tile(CELLS + c)
        at = moved_ref[c] if second else tile
        points = at + centre
        row = rows_of(points.shape)
        core = tile[3:4, :]
        half = 0.5 * core * core
        pos = jnp.where(row < 3, points, 0.0)
        norm = jnp.sum(pos * pos, axis=0, keepdims=True) + half
        value = jnp.where(
            row == 3, 1.0, jnp.where(row == 4, norm, jnp.where(row == 5, half, -2.0 * pos))
        )
        high, mid, low = split3(value)
        stack = jnp.concatenate([high, mid, high, mid, low, high], axis=0)
        stack = jnp.concatenate([stack, jnp.zeros((SLOTS - FEATS, SLOTS), F32)], axis=0)
        targ[c] = stack.T.astype(BF16)
        return 0

    lax.fori_loop(0, CELLS, target_prep, 0)

    if not second:
        far_pad = jnp.concatenate(
            [far_ref[...].astype(F32), jnp.full((3, CELLS), -1.0, F32)], axis=0
        )
        far_pad = jnp.concatenate([far_pad, jnp.full((256 - 192, CELLS), -1.0, F32)], axis=0)
        far_pad = jnp.concatenate([far_pad, jnp.full((256, SLOTS - CELLS), -1.0, F32)], axis=1)
        acc[...] = jnp.concatenate([far_pad[0:128].T, far_pad[128:256].T], axis=1)[0:CELLS]
        table = table_ref[...].reshape(2 * N * 3 * N, SLOTS)
        table_high = table.astype(BF16)
        table_low = (table - table_high.astype(F32)).astype(BF16)
        table2 = jnp.concatenate([table_high, table_low], axis=1)

        def far_gather(c, _):
            ids = acc[pl.ds(c, 1), :].astype(jnp.int32)
            lane_hot = jnp.where(rows_of((SLOTS, 256)) == (ids & 127), 1.0, 0.0).astype(BF16)
            got = nn(table2, jnp.concatenate([lane_hot, lane_hot], axis=0))
            high = ids >> 7
            sums = [jnp.zeros((8, 256), F32) for _ in range(3)]
            for g in range(2 * N):
                start = (g % 2) * N * 3 * N + (g // 2) * 3 * N
                here = rows_of((8, 256)) + g * N == high
                for comp in range(3):
                    part = got[start + comp * N : start + comp * N + N]
                    sums[comp] = sums[comp] + jnp.where(here, part, 0.0)
            strength = [jnp.sum(s, axis=0, keepdims=True) for s in sums]
            spots = axis_bits(jnp.broadcast_to(jnp.maximum(ids, 0), (8, 256)))
            points = (spots - jnp.concatenate([base, base], axis=1)).astype(F32)
            row = rows_of(points.shape)
            tile = jnp.where(row < 3, points, 0.0)
            for comp in range(3):
                tile = jnp.where(row == 5 + comp, strength[comp], tile)
            far_out[2 * c] = tile[:, :SLOTS]
            far_out[2 * c + 1] = tile[:, SLOTS:]
            return 0

        lax.fori_loop(0, CELLS, far_gather, 0)
        far = far_out
    else:
        far = far_in

    def far_prep(i, _):
        tile = far[i]
        put(FAR_BASE + i, source_rows(tile, 0.0, 1.0), tile)
        weight[FAR_BASE + i] = moments(
            (tile[0:1], tile[1:2], tile[2:3]), (tile[5:6], tile[6:7], tile[7:8])
        )
        return 0

    lax.fori_loop(0, 2 * CELLS, far_prep, 0)

    for c in range(CELLS):
        used = jnp.int32(0)
        for e in range(NEAR):
            used = used + jnp.where(near_ref[e, c] >= 0, 1, 0)
        count[c] = used

    first_near = base_id - CELLS

    def pair(target, one, two):
        features = jnp.concatenate([feat[one], feat[two]], axis=1)
        features = jnp.concatenate(
            [features, jnp.zeros((SLOTS - FEATS, 2 * SLOTS), BF16)], axis=0
        )
        dist = jnp.maximum(nn(target, features), 0.08)
        root = lax.rsqrt(dist)
        q = root * root * root
        q_high = q.astype(BF16)
        q_low = (q - q_high.astype(F32)).astype(BF16)
        w = jnp.concatenate([weight[one], weight[two]], axis=1)
        return nt(q_high, w) + nt(q_low, w)

    def cell(c, _):
        target = targ[c]
        total = pair(target, FAR_BASE + 2 * c, FAR_BASE + 2 * c + 1)
        used = count[c]

        def step(p, total):
            one = near_ref[2 * p, c] - first_near
            two = jnp.where(2 * p + 1 < used, near_ref[2 * p + 1, c] - first_near, DUMMY)
            return total + pair(target, one, two)

        total = lax.fori_loop(0, (used + 1) // 2, step, total)
        full = jnp.concatenate([total, jnp.zeros((SLOTS, SLOTS - 16), F32)], axis=1).T
        sums = full[0:8] + full[8:16]
        tile, centre = own_tile(CELLS + c)
        at = moved_ref[c] if second else tile
        points = at + centre
        px, py, pz = points[0:1], points[1:2], points[2:3]
        bx, by, bz, ax, ay, az = (sums[r : r + 1] for r in range(6))
        row = rows_of((8, SLOTS))
        vel = jnp.where(
            row == 0, by * pz - bz * py - ax,
            jnp.where(row == 1, bz * px - bx * pz - ay, bx * py - by * px - az),
        )
        vel = jnp.where((row < 3) & (tile[4:5] > 0.0), vel, 0.0)
        if second:
            out_ref[c] = 0.5 * (first_ref[c] + vel)
        else:
            first_ref[c] = vel
            moved_ref[c] = jnp.where(row < 3, tile + 0.25 * vel, 0.0)
        return 0

    lax.fori_loop(0, CELLS, cell, 0)


def run_pass(second, near_list, own_base, ext, *more):
    vmem = pl.BlockSpec(memory_space=pltpu.VMEM)
    smem = pl.BlockSpec(memory_space=pltpu.SMEM)
    tiles = jax.ShapeDtypeStruct((CELLS, 8, SLOTS), F32)
    outs = tiles if second else (tiles, tiles, jax.ShapeDtypeStruct((2 * CELLS, 8, SLOTS), F32))
    return pl.pallas_call(
        functools.partial(pass_kernel, second),
        out_shape=outs,
        in_specs=[smem, smem, vmem] + [vmem] * len(more),
        out_specs=vmem if second else (vmem,) * 3,
        scratch_shapes=[
            pltpu.VMEM((CHUNKS, FEATS, SLOTS), BF16),
            pltpu.VMEM((CHUNKS, 16, SLOTS), BF16),
            pltpu.VMEM((CELLS, SLOTS, SLOTS), BF16),
            pltpu.SMEM((CELLS,), jnp.int32),
            pltpu.VMEM((CELLS, 2 * SLOTS), F32),
        ],
        compiler_params=pltpu.CompilerParams(vmem_limit_bytes=40 * 1024 * 1024),
    )(near_list, own_base, ext, *more)


def route(offsets, strengths, cores, place):
    vmem = pl.BlockSpec(memory_space=pltpu.VMEM)
    sems = [pltpu.SemaphoreType.DMA((N,))] * 4 + [pltpu.SemaphoreType.DMA((2,))] * 2
    sems = sems + [pltpu.SemaphoreType.DMA((N,))] * 8
    return pl.pallas_call(
        route_kernel,
        out_shape=(
            jax.ShapeDtypeStruct((3 * CELLS, 8, SLOTS), F32),
            jax.ShapeDtypeStruct((2, N, 3, N, SLOTS), F32),
        ),
        in_specs=[vmem] * 4,
        out_specs=(vmem, vmem),
        scratch_shapes=[
            pltpu.VMEM((8, offsets.shape[1]), F32),
            pltpu.VMEM((256, 2 * N * SLOTS), BF16),
            pltpu.VMEM((2 * N, 8, SLOTS), F32),
            pltpu.VMEM((N, 2, 8, SLOTS), F32),
            pltpu.VMEM((N, 2, 8, SLOTS), F32),
            pltpu.VMEM((N, 2, 8, SLOTS), F32),
            pltpu.VMEM((8, SLOTS), F32),
            pltpu.VMEM((N, 8, SLOTS), F32),
            pltpu.VMEM((N, 8, SLOTS), F32),
        ] + sems,
        compiler_params=pltpu.CompilerParams(
            collective_id=0, has_side_effects=True, vmem_limit_bytes=40 * 1024 * 1024
        ),
    )(offsets, strengths, cores.reshape(1, -1), place)


def exchange(moved):
    vmem = pl.BlockSpec(memory_space=pltpu.VMEM)
    return pl.pallas_call(
        halo_kernel,
        out_shape=jax.ShapeDtypeStruct((2, CELLS, 8, SLOTS), F32),
        in_specs=[vmem],
        out_specs=vmem,
        scratch_shapes=[pltpu.SemaphoreType.DMA((2,)), pltpu.SemaphoreType.DMA((2,))],
        compiler_params=pltpu.CompilerParams(collective_id=1, has_side_effects=True),
    )(moved)


def per_device(offsets, strengths, cores, place, near_list, far_list):
    device = lax.axis_index("grp") * (N * N) + lax.axis_index("dev")
    own_base = (device * CELLS).astype(jnp.int32).reshape(1)
    ext, table = route(offsets, strengths, cores, place)
    first, moved, far = run_pass(False, near_list, own_base, ext, table, far_list)
    move = exchange(moved)
    out = run_pass(True, near_list, own_base, ext, move, moved, first, far)
    return jnp.transpose(out[:, 0:3], (1, 0, 2)).reshape(3, CELLS * SLOTS)


def solution(mesh):
    row = P(None, ("grp", "dev"))
    return jax.shard_map(
        per_device, mesh=mesh, in_specs=(row, row, P(("grp", "dev")), row, row, row),
        out_specs=row, check_vma=False,
    )
```

```python
import functools
import math

import jax
import jax.numpy as jnp
from jax import lax
from jax.experimental import pallas as pl
from jax.experimental.pallas import tpu as pltpu
from jax.sharding import PartitionSpec as P

SLOTS = 128
CELLS = 16
CAP = 32
NEAR = 14
FAR = 189
N = 8
INV_FOUR_PI = 0.25 / math.pi
MESH = pl.DeviceIdType.MESH
F32 = jnp.float32
BF16 = jnp.bfloat16

NEAR_CHUNKS = 3 * CELLS
DUMMY = NEAR_CHUNKS
FAR_BASE = NEAR_CHUNKS + 2
CHUNKS = FAR_BASE + 2 * CELLS
FEATS = 48
UNROLL = 8


def nt(a, b):
    return lax.dot_general(a, b, (((1,), (1,)), ((), ())), preferred_element_type=F32)


def nn(a, b):
    return lax.dot_general(a, b, (((1,), (0,)), ((), ())), preferred_element_type=F32)


def rows_of(shape):
    return lax.broadcasted_iota(jnp.int32, shape, len(shape) - 2)


def lanes_of(shape):
    return lax.broadcasted_iota(jnp.int32, shape, len(shape) - 1)


def split2(value):
    high = value.astype(BF16).astype(F32)
    return jnp.concatenate([high, value - high], axis=0)


def route_kernel(
    off_ref, str_ref, core_ref, place_ref, ext_ref, table_ref,
    fields, spread, send1, recv1, send2, recv2, sums_x, sums_y,
    sx_s, sx_r, sy_s, sy_r, halo_s, halo_r, cy_s, cy_r, cx_s, cx_r, cz_s, cz_r, cc_s, cc_r,
):
    dev = lax.axis_index("dev")
    grp = lax.axis_index("grp")
    x, y = dev // N, dev % N
    z, core = grp // 2, grp % 2

    def x_peer(k):
        return (x + k) % N

    def y_peer(k):
        return (y + k) % N

    def z_peer(k):
        return (z + k) % N

    right, left = (dev + 1) % (N * N), (dev + N * N - 1) % (N * N)
    barrier = pltpu.get_barrier_semaphore()
    for k in range(1, N):
        pl.semaphore_signal(barrier, 1, device_id={"dev": x_peer(k) * N + y}, device_id_type=MESH)
        pl.semaphore_signal(barrier, 1, device_id={"dev": x * N + y_peer(k)}, device_id_type=MESH)
        pl.semaphore_signal(barrier, 1, device_id={"grp": z_peer(k) * 2 + core}, device_id_type=MESH)
    pl.semaphore_signal(barrier, 1, device_id={"dev": right}, device_id_type=MESH)
    pl.semaphore_signal(barrier, 1, device_id={"dev": left}, device_id_type=MESH)
    pl.semaphore_signal(barrier, 1, device_id={"grp": z * 2 + (1 - core)}, device_id_type=MESH)

    rows = off_ref.shape[1]
    cell_row = place_ref[0:1, :]
    spot = (cell_row & (CELLS - 1)) * SLOTS + place_ref[1:2, :] + 1
    owner = (cell_row >> 4) & (N * N - 1)
    fields[0:3, :] = off_ref[...]
    fields[3:4, :] = core_ref[...]
    fields[4:5, :] = spot.astype(F32)
    fields[5:8, :] = str_ref[...]
    both = split2(fields[...])
    earlier = rows_of((SLOTS, 2 * SLOTS)) < lanes_of((SLOTS, 2 * SLOTS))
    counter = jnp.where(earlier | (lanes_of((SLOTS, 2 * SLOTS)) >= SLOTS), 1.0, 0.0).astype(BF16)
    carry = jnp.zeros((N * N, SLOTS), F32)
    ranks = []
    for b in range(rows // SLOTS):
        hot = jnp.where(rows_of((N * N, SLOTS)) == owner[:, b * SLOTS : (b + 1) * SLOTS], 1.0, 0.0)
        count = nn(hot.astype(BF16), counter)
        ranks.append(jnp.sum(hot * (count[:, :SLOTS] + carry), axis=0, keepdims=True))
        carry = carry + count[:, SLOTS:]
    rank = jnp.concatenate(ranks, axis=1).astype(jnp.int32)
    low = (owner & 3) * CAP + rank
    high = owner >> 2
    low_hot = jnp.where(rows_of((SLOTS, rows)) == low, 1.0, 0.0).astype(BF16)
    for t in range(2 * N):
        spread[16 * t : 16 * t + 16, 0:rows] = jnp.where(high == t, both, 0.0).astype(BF16)
    packed = nt(spread[:, 0:rows], low_hot)
    for t in range(2 * N):
        send1[t] = packed[16 * t : 16 * t + 8] + packed[16 * t + 8 : 16 * t + 16]

    owner_x = owner >> 3
    shares = jnp.concatenate(
        [jnp.where(rows_of((8, rows)) == owner_x, both[r : r + 1], 0.0) for r in (5, 6, 7, 13, 14, 15)],
        axis=0,
    ).astype(BF16)
    lane_hot = jnp.where(rows_of((SLOTS, rows)) == (cell_row & (SLOTS - 1)), 1.0, 0.0).astype(BF16)
    share = nt(shares, lane_hot)
    for comp in range(3):
        sums_x[x, comp] = share[8 * comp : 8 * comp + 8] + share[24 + 8 * comp : 32 + 8 * comp]

    pl.semaphore_wait(barrier, 3 * (N - 1) + 3)

    copies = []
    for k in range(1, N):
        to = x_peer(k)
        copy = pltpu.make_async_remote_copy(
            src_ref=send1.at[pl.ds(2 * to, 2)], dst_ref=recv1.at[x],
            send_sem=sx_s.at[k], recv_sem=sx_r.at[k],
            device_id={"dev": to * N + y}, device_id_type=MESH,
        )
        copy.start()
        copies.append(copy)
    x_copies = []
    for k in range(1, N):
        copy = pltpu.make_async_remote_copy(
            src_ref=sums_x.at[x], dst_ref=sums_x.at[x],
            send_sem=cx_s.at[k], recv_sem=cx_r.at[k],
            device_id={"dev": x_peer(k) * N + y}, device_id_type=MESH,
        )
        copy.start()
        x_copies.append(copy)
    recv1[x] = send1[pl.ds(2 * x, 2)]
    for copy in copies:
        copy.wait_recv()
    lane_group = lanes_of((8, SLOTS)) // CAP
    for t in range(N):
        for k in range(2):
            tile = None
            for g in range(4):
                part = recv1[4 * k + g, t // 4]
                turn = (g - t % 4) % 4 * CAP
                if turn:
                    part = pltpu.roll(part, turn, 1)
                tile = part if tile is None else jnp.where(lane_group == g, part, tile)
            send2[t, k] = tile
    for k in range(1, N):
        to = y_peer(k)
        copy = pltpu.make_async_remote_copy(
            src_ref=send2.at[to], dst_ref=recv2.at[y],
            send_sem=sy_s.at[k], recv_sem=sy_r.at[k],
            device_id={"dev": x * N + to}, device_id_type=MESH,
        )
        copy.start()
        copies.append(copy)
    for copy in x_copies:
        copy.wait_recv()
    total = sums_x[0]
    for k in range(1, N):
        total = total + sums_x[k]
    sums_y[y] = total
    sum_copies = []
    for k in range(1, N):
        copy = pltpu.make_async_remote_copy(
            src_ref=sums_y.at[y], dst_ref=sums_y.at[y],
            send_sem=cy_s.at[k], recv_sem=cy_r.at[k],
            device_id={"dev": x * N + y_peer(k)}, device_id_type=MESH,
        )
        copy.start()
        sum_copies.append(copy)
    recv2[y] = send2[y]
    for copy in sum_copies:
        copy.wait_recv()
    total = sums_y[0]
    for k in range(1, N):
        total = total + sums_y[k]
    table_ref[core, z] = total
    z_copies = []
    for k in range(1, N):
        copy = pltpu.make_async_remote_copy(
            src_ref=table_ref.at[core, z], dst_ref=table_ref.at[core, z],
            send_sem=cz_s.at[k], recv_sem=cz_r.at[k],
            device_id={"grp": z_peer(k) * 2 + core}, device_id_type=MESH,
        )
        copy.start()
        z_copies.append(copy)
    for copy in copies[N - 1 :]:
        copy.wait_recv()

    slot_rows = []
    for t in range(2 * N):
        tile = recv2[t // 2, t % 2]
        spot_row = tile[4:5, :] - 1.0
        cell = jnp.floor(spot_row * (1.0 / SLOTS))
        slot = (spot_row - cell * SLOTS).astype(jnp.int32)
        cell = cell.astype(jnp.int32)
        two = split2(tile)
        slot_rows.append(jnp.where(rows_of((SLOTS, SLOTS)) == slot, 1.0, 0.0).astype(BF16))
        for c in range(CELLS):
            spread[16 * c : 16 * c + 16, t * SLOTS : (t + 1) * SLOTS] = jnp.where(
                cell == c, two, 0.0
            ).astype(BF16)
    placed = nt(spread[...], jnp.concatenate(slot_rows, axis=1))
    for c in range(CELLS):
        tile = placed[16 * c : 16 * c + 8] + placed[16 * c + 8 : 16 * c + 16]
        empty = (rows_of((8, SLOTS)) == 3) & (tile[4:5, :] == 0.0)
        ext_ref[CELLS + c] = jnp.where(empty, 1.0, tile)

    halo = []
    for i, (to, at) in enumerate(((right, 0), (left, 2 * CELLS))):
        copy = pltpu.make_async_remote_copy(
            src_ref=ext_ref.at[pl.ds(CELLS, CELLS)], dst_ref=ext_ref.at[pl.ds(at, CELLS)],
            send_sem=halo_s.at[i], recv_sem=halo_r.at[i],
            device_id={"dev": to}, device_id_type=MESH,
        )
        copy.start()
        halo.append(copy)

    core_copies = []
    for k in range(N):
        if k:
            z_copies[k - 1].wait_recv()
        source = (z + N - k) % N
        copy = pltpu.make_async_remote_copy(
            src_ref=table_ref.at[core, source], dst_ref=table_ref.at[core, source],
            send_sem=cc_s.at[k], recv_sem=cc_r.at[k],
            device_id={"grp": z * 2 + (1 - core)}, device_id_type=MESH,
        )
        copy.start()
        core_copies.append(copy)
    for copy in core_copies + halo:
        copy.wait_recv()
    for copy in copies + sum_copies + x_copies + z_copies + core_copies + halo:
        copy.wait_send()


def halo_kernel(moved_ref, ext_ref, send_sem, recv_sem):
    dev = lax.axis_index("dev")
    right, left = (dev + 1) % (N * N), (dev + N * N - 1) % (N * N)
    barrier = pltpu.get_barrier_semaphore()
    for to in (right, left):
        pl.semaphore_signal(barrier, 1, device_id={"dev": to}, device_id_type=MESH)
    pl.semaphore_wait(barrier, 2)
    halo = []
    for i, to in enumerate((right, left)):
        copy = pltpu.make_async_remote_copy(
            src_ref=moved_ref, dst_ref=ext_ref.at[i],
            send_sem=send_sem.at[i], recv_sem=recv_sem.at[i],
            device_id={"dev": to}, device_id_type=MESH,
        )
        copy.start()
        halo.append(copy)
    for copy in halo:
        copy.wait()


def loop(count, at_once, body):
    def several(i, _):
        for u in range(at_once):
            body(i * at_once + u, 0)
        return 0

    lax.fori_loop(0, count // at_once, several, 0)


def axis_bits(ids):
    shifted = ids >> jnp.minimum(rows_of(ids.shape), 2)
    value = shifted & 1
    for bit in range(1, 5):
        value = value + ((shifted >> (3 * bit)) & 1) * (1 << bit)
    return value


def source_rows(points, half, flag):
    row = rows_of(points.shape)
    at = jnp.where(row < 3, points, 0.0)
    norm = jnp.sum(at * at, axis=0, keepdims=True) + half
    return jnp.where(row == 3, norm, jnp.where(row == 4, 1.0, jnp.where(row == 5, flag, at)))


def split3(tile):
    high = tile.astype(BF16).astype(F32)
    rest = tile - high
    mid = rest.astype(BF16).astype(F32)
    return high, mid, rest - mid


def moments(points, strength):
    sx, sy, sz = (INV_FOUR_PI * s for s in strength)
    px, py, pz = points
    row = rows_of((8, sx.shape[1]))
    tile = jnp.zeros((8, sx.shape[1]), F32)
    values = (sx, sy, sz, sy * pz - sz * py, sz * px - sx * pz, sx * py - sy * px)
    for r, value in enumerate(values):
        tile = jnp.where(row == r, value, tile)
    return split2(tile).astype(BF16)


def pass_kernel(
    second, near_ref, own_ref, ext_ref, *rest
):
    if second:
        move_ref, moved_ref, first_ref, far_in, out_ref, feat, weight, targ, far_ids, step_cell, step_one, step_two, acc = rest
    else:
        table_ref, far_ref, first_ref, moved_ref, far_out, feat, weight, targ, far_ids, step_cell, step_one, step_two, acc = rest
    base_id = own_ref[0]
    base = axis_bits(jnp.full((8, SLOTS), base_id, jnp.int32))

    def put(chunk, tile):
        high, mid, low = split3(tile)
        feat[chunk] = jnp.concatenate([high, high, mid, mid, high, low], axis=0).astype(BF16)

    def own_tile(l):
        tile = ext_ref[l]
        ids = jnp.full((8, SLOTS), base_id - CELLS + l, jnp.int32)
        centre = (axis_bits(ids) - base).astype(F32)
        return tile, centre

    def near_prep(l, _):
        tile, centre = own_tile(l)
        at = tile
        if second:
            side = l // CELLS
            within = l - side * CELLS
            at = jnp.where(
                side == 1, moved_ref[within],
                jnp.where(side == 0, move_ref[0, within], move_ref[1, within]),
            )
        points = at + centre
        core = tile[3:4, :]
        half = 0.5 * core * core
        put(l, source_rows(points, half, 0.0))
        weight[l] = moments(
            (points[0:1], points[1:2], points[2:3]), (tile[5:6], tile[6:7], tile[7:8])
        )

    loop(NEAR_CHUNKS, 8, near_prep)
    targ[CELLS] = jnp.zeros((SLOTS, FEATS), BF16)
    feat[DUMMY] = jnp.zeros((FEATS, SLOTS), BF16)
    weight[DUMMY] = jnp.zeros((16, SLOTS), BF16)

    def target_prep(c, _):
        tile, centre = own_tile(CELLS + c)
        at = moved_ref[c] if second else tile
        points = at + centre
        row = rows_of(points.shape)
        core = tile[3:4, :]
        half = 0.5 * core * core
        pos = jnp.where(row < 3, points, 0.0)
        norm = jnp.sum(pos * pos, axis=0, keepdims=True) + half
        value = jnp.where(
            row == 3, 1.0, jnp.where(row == 4, norm, jnp.where(row == 5, half, -2.0 * pos))
        )
        high, mid, low = split3(value)
        stack = jnp.concatenate([high, mid, high, mid, low, high], axis=0)
        stack = jnp.concatenate([stack, jnp.zeros((SLOTS - FEATS, SLOTS), F32)], axis=0)
        targ[c] = stack.T[:, :FEATS].astype(BF16)

    loop(CELLS, 4, target_prep)

    if not second:
        far_pad = jnp.concatenate(
            [far_ref[...].astype(F32), jnp.full((3, CELLS), -1.0, F32)], axis=0
        )
        far_pad = jnp.concatenate([far_pad, jnp.full((256 - 192, CELLS), -1.0, F32)], axis=0)
        far_pad = jnp.concatenate([far_pad, jnp.full((256, SLOTS - CELLS), -1.0, F32)], axis=1)
        far_ids[...] = jnp.concatenate([far_pad[0:128].T, far_pad[128:256].T], axis=1)[0:CELLS]
        table = table_ref[...].reshape(2 * N * 3 * N, SLOTS)
        table_high = table.astype(BF16)
        table_low = (table - table_high.astype(F32)).astype(BF16)
        table2 = jnp.concatenate([table_high, table_low], axis=1)

        def far_gather(c, _):
            ids = far_ids[pl.ds(c, 1), :].astype(jnp.int32)
            lane_hot = jnp.where(rows_of((SLOTS, 256)) == (ids & 127), 1.0, 0.0).astype(BF16)
            got = nn(table2, jnp.concatenate([lane_hot, lane_hot], axis=0))
            high = ids >> 7
            sums = [jnp.zeros((8, 256), F32) for _ in range(3)]
            for g in range(2 * N):
                start = (g % 2) * N * 3 * N + (g // 2) * 3 * N
                here = rows_of((8, 256)) + g * N == high
                for comp in range(3):
                    part = got[start + comp * N : start + comp * N + N]
                    sums[comp] = sums[comp] + jnp.where(here, part, 0.0)
            strength = [jnp.sum(s, axis=0, keepdims=True) for s in sums]
            spots = axis_bits(jnp.broadcast_to(jnp.maximum(ids, 0), (8, 256)))
            points = (spots - jnp.concatenate([base, base], axis=1)).astype(F32)
            row = rows_of(points.shape)
            tile = jnp.where(row < 3, points, 0.0)
            for comp in range(3):
                tile = jnp.where(row == 5 + comp, strength[comp], tile)
            far_out[2 * c] = tile[:, :SLOTS]
            far_out[2 * c + 1] = tile[:, SLOTS:]

        loop(CELLS, 2, far_gather)
        far = far_out
    else:
        far = far_in

    def far_prep(i, _):
        tile = far[i]
        put(FAR_BASE + i, source_rows(tile, 0.0, 1.0))
        weight[FAR_BASE + i] = moments(
            (tile[0:1], tile[1:2], tile[2:3]), (tile[5:6], tile[6:7], tile[7:8])
        )

    loop(2 * CELLS, 8, far_prep)

    first_near = base_id - CELLS
    total = jnp.int32(CELLS)
    for c in range(CELLS):
        step_cell[c] = c
        step_one[c] = FAR_BASE + 2 * c
        step_two[c] = FAR_BASE + 2 * c + 1
    for c in range(CELLS):
        for p in range(NEAR // 2):
            one, two = near_ref[2 * p, c], near_ref[2 * p + 1, c]
            step_cell[total] = c
            step_one[total] = one - first_near
            step_two[total] = jnp.where(two >= 0, two - first_near, DUMMY)
            total = total + jnp.where(one >= 0, 1, 0)
    for p in range(UNROLL):
        step_cell[total + p] = CELLS
        step_one[total + p] = DUMMY
        step_two[total + p] = DUMMY
    acc[...] = jnp.zeros(acc.shape, F32)

    def distances(target, one, two):
        features = jnp.concatenate([feat[one], feat[two]], axis=1)
        return nn(target, features)

    def powers(dist):
        root = lax.rsqrt(jnp.maximum(dist, 0.08))
        q = root * root * root
        q_high = q.astype(BF16)
        return q_high, (q - q_high.astype(F32)).astype(BF16)

    def sums_of(high, low, one, two):
        w = jnp.concatenate([weight[one], weight[two]], axis=1)
        return nt(high, w) + nt(low, w)

    def steps(i, _):
        at = [i * UNROLL + u for u in range(UNROLL)]
        cells = [step_cell[p] for p in at]
        ones = [step_one[p] for p in at]
        twos = [step_two[p] for p in at]
        dists = [distances(targ[cells[u]], ones[u], twos[u]) for u in range(UNROLL)]
        qs = [powers(d) for d in dists]
        parts = [sums_of(*qs[u], ones[u], twos[u]) for u in range(UNROLL)]
        for u in range(UNROLL):
            acc[cells[u]] += parts[u]
        return 0

    lax.fori_loop(0, (total + UNROLL - 1) // UNROLL, steps, 0)

    def cell(c, _):
        full = jnp.concatenate([acc[c], jnp.zeros((SLOTS, SLOTS - 16), F32)], axis=1).T
        sums = full[0:8] + full[8:16]
        tile, centre = own_tile(CELLS + c)
        at = moved_ref[c] if second else tile
        points = at + centre
        px, py, pz = points[0:1], points[1:2], points[2:3]
        bx, by, bz, ax, ay, az = (sums[r : r + 1] for r in range(6))
        row = rows_of((8, SLOTS))
        vel = jnp.where(
            row == 0, by * pz - bz * py - ax,
            jnp.where(row == 1, bz * px - bx * pz - ay, bx * py - by * px - az),
        )
        vel = jnp.where((row < 3) & (tile[4:5] > 0.0), vel, 0.0)
        if second:
            out_ref[c] = 0.5 * (first_ref[c] + vel)
        else:
            first_ref[c] = vel
            moved_ref[c] = jnp.where(row < 3, tile + 0.25 * vel, 0.0)

    loop(CELLS, 4, cell)


def run_pass(second, near_list, own_base, ext, *more):
    vmem = pl.BlockSpec(memory_space=pltpu.VMEM)
    smem = pl.BlockSpec(memory_space=pltpu.SMEM)
    tiles = jax.ShapeDtypeStruct((CELLS, 8, SLOTS), F32)
    outs = tiles if second else (tiles, tiles, jax.ShapeDtypeStruct((2 * CELLS, 8, SLOTS), F32))
    return pl.pallas_call(
        functools.partial(pass_kernel, second),
        out_shape=outs,
        in_specs=[smem, smem, vmem] + [vmem] * len(more),
        out_specs=vmem if second else (vmem,) * 3,
        scratch_shapes=[
            pltpu.VMEM((CHUNKS, FEATS, SLOTS), BF16),
            pltpu.VMEM((CHUNKS, 16, SLOTS), BF16),
            pltpu.VMEM((CELLS + 1, SLOTS, FEATS), BF16),
            pltpu.VMEM((CELLS, 2 * SLOTS), F32),
            pltpu.SMEM((CELLS * 8 + UNROLL,), jnp.int32),
            pltpu.SMEM((CELLS * 8 + UNROLL,), jnp.int32),
            pltpu.SMEM((CELLS * 8 + UNROLL,), jnp.int32),
            pltpu.VMEM((CELLS + 1, SLOTS, 16), F32),
        ],
        compiler_params=pltpu.CompilerParams(vmem_limit_bytes=40 * 1024 * 1024),
    )(near_list, own_base, ext, *more)


def route(offsets, strengths, cores, place):
    vmem = pl.BlockSpec(memory_space=pltpu.VMEM)
    sems = [pltpu.SemaphoreType.DMA((N,))] * 4 + [pltpu.SemaphoreType.DMA((2,))] * 2
    sems = sems + [pltpu.SemaphoreType.DMA((N,))] * 8
    return pl.pallas_call(
        route_kernel,
        out_shape=(
            jax.ShapeDtypeStruct((3 * CELLS, 8, SLOTS), F32),
            jax.ShapeDtypeStruct((2, N, 3, N, SLOTS), F32),
        ),
        in_specs=[vmem] * 4,
        out_specs=(vmem, vmem),
        scratch_shapes=[
            pltpu.VMEM((8, offsets.shape[1]), F32),
            pltpu.VMEM((256, 2 * N * SLOTS), BF16),
            pltpu.VMEM((2 * N, 8, SLOTS), F32),
            pltpu.VMEM((N, 2, 8, SLOTS), F32),
            pltpu.VMEM((N, 2, 8, SLOTS), F32),
            pltpu.VMEM((N, 2, 8, SLOTS), F32),
            pltpu.VMEM((N, 3, N, SLOTS), F32),
            pltpu.VMEM((N, 3, N, SLOTS), F32),
        ] + sems,
        compiler_params=pltpu.CompilerParams(
            collective_id=0, has_side_effects=True, vmem_limit_bytes=40 * 1024 * 1024
        ),
    )(offsets, strengths, cores.reshape(1, -1), place)


def exchange(moved):
    vmem = pl.BlockSpec(memory_space=pltpu.VMEM)
    return pl.pallas_call(
        halo_kernel,
        out_shape=jax.ShapeDtypeStruct((2, CELLS, 8, SLOTS), F32),
        in_specs=[vmem],
        out_specs=vmem,
        scratch_shapes=[pltpu.SemaphoreType.DMA((2,)), pltpu.SemaphoreType.DMA((2,))],
        compiler_params=pltpu.CompilerParams(collective_id=1, has_side_effects=True),
    )(moved)


def per_device(offsets, strengths, cores, place, near_list, far_list):
    device = lax.axis_index("grp") * (N * N) + lax.axis_index("dev")
    own_base = (device * CELLS).astype(jnp.int32).reshape(1)
    ext, table = route(offsets, strengths, cores, place)
    first, moved, far = run_pass(False, near_list, own_base, ext, table, far_list)
    move = exchange(moved)
    out = run_pass(True, near_list, own_base, ext, move, moved, first, far)
    return jnp.transpose(out[:, 0:3], (1, 0, 2)).reshape(3, CELLS * SLOTS)


def solution(mesh):
    row = P(None, ("grp", "dev"))
    return jax.shard_map(
        per_device, mesh=mesh, in_specs=(row, row, P(("grp", "dev")), row, row, row),
        out_specs=row, check_vma=False,
    )
```

```python
import functools
import math

import jax
import jax.numpy as jnp
from jax import lax
from jax.experimental import pallas as pl
from jax.experimental.pallas import tpu as pltpu
from jax.sharding import PartitionSpec as P

SLOTS = 128
CELLS = 16
CAP = 32
NEAR = 14
FAR = 189
N = 8
INV_FOUR_PI = 0.25 / math.pi
MESH = pl.DeviceIdType.MESH
F32 = jnp.float32
BF16 = jnp.bfloat16

NEAR_CHUNKS = 3 * CELLS
DUMMY = NEAR_CHUNKS
FAR_BASE = NEAR_CHUNKS + 2
CHUNKS = FAR_BASE + 2 * CELLS
FEATS = 48
HALF = SLOTS // 2
LIST = 40
UNROLL = 12
FAR_FIRST = (4, 3, 5, 2, 6, 1, 7)


def nt(a, b):
    return lax.dot_general(a, b, (((1,), (1,)), ((), ())), preferred_element_type=F32)


def nn(a, b):
    return lax.dot_general(a, b, (((1,), (0,)), ((), ())), preferred_element_type=F32)


def rows_of(shape):
    return lax.broadcasted_iota(jnp.int32, shape, len(shape) - 2)


def lanes_of(shape):
    return lax.broadcasted_iota(jnp.int32, shape, len(shape) - 1)


def split2(value):
    high = value.astype(BF16).astype(F32)
    return jnp.concatenate([high, value - high], axis=0)


def route_kernel(
    rows_ref, ext_ref, table_ref, fields, spread, send1, recv1, send2, recv2,
    sx_s, sx_r, sy_s, sy_r, cz_s, cz_r, halo_s, halo_r, cc_s, cc_r,
):
    dev = lax.axis_index("dev")
    grp = lax.axis_index("grp")
    x, y = dev // N, dev % N
    z, core = grp // 2, grp % 2

    def x_peer(k):
        return (x + k) % N

    def y_peer(k):
        return (y + k) % N

    def z_peer(k):
        return (z + k) % N

    right, left = (dev + 1) % (N * N), (dev + N * N - 1) % (N * N)
    barrier = pltpu.get_barrier_semaphore()
    for k in range(1, N):
        pl.semaphore_signal(barrier, 1, device_id={"dev": x_peer(k) * N + y}, device_id_type=MESH)
        pl.semaphore_signal(barrier, 1, device_id={"dev": x * N + y_peer(k)}, device_id_type=MESH)
        pl.semaphore_signal(barrier, 1, device_id={"grp": z_peer(k) * 2 + core}, device_id_type=MESH)
    pl.semaphore_signal(barrier, 1, device_id={"dev": right}, device_id_type=MESH)
    pl.semaphore_signal(barrier, 1, device_id={"dev": left}, device_id_type=MESH)
    pl.semaphore_signal(barrier, 1, device_id={"grp": z * 2 + (1 - core)}, device_id_type=MESH)

    rows = rows_ref.shape[1]
    place = rows_ref[4:5, :].astype(jnp.int32)
    cell_row = place >> 7
    spot = (place & (CELLS * SLOTS - 1)) + 1
    owner = (cell_row >> 4) & (N * N - 1)
    fields[...] = jnp.where(rows_of((8, rows)) == 4, spot.astype(F32), rows_ref[...])
    both = split2(fields[...])
    earlier = rows_of((SLOTS, 2 * SLOTS)) < lanes_of((SLOTS, 2 * SLOTS))
    counter = jnp.where(earlier | (lanes_of((SLOTS, 2 * SLOTS)) >= SLOTS), 1.0, 0.0).astype(BF16)
    carry = jnp.zeros((N * N, SLOTS), F32)
    ranks = []
    for b in range(rows // SLOTS):
        hot = jnp.where(rows_of((N * N, SLOTS)) == owner[:, b * SLOTS : (b + 1) * SLOTS], 1.0, 0.0)
        count = nn(hot.astype(BF16), counter)
        ranks.append(jnp.sum(hot * (count[:, :SLOTS] + carry), axis=0, keepdims=True))
        carry = carry + count[:, SLOTS:]
    rank = jnp.concatenate(ranks, axis=1).astype(jnp.int32)
    low = (owner & 3) * CAP + rank
    high = owner >> 2
    low_hot = jnp.where(rows_of((SLOTS, rows)) == low, 1.0, 0.0).astype(BF16)
    for t in range(2 * N):
        spread[16 * t : 16 * t + 16, 0:rows] = jnp.where(high == t, both, 0.0).astype(BF16)
    packed = nt(spread[:, 0:rows], low_hot)
    for t in range(2 * N):
        send1[t // 2, t % 2] = packed[16 * t : 16 * t + 8] + packed[16 * t + 8 : 16 * t + 16]

    owner_x = owner >> 3
    shares = jnp.concatenate(
        [jnp.where(rows_of((8, rows)) == owner_x, both[r : r + 1], 0.0) for r in (5, 6, 7, 13, 14, 15)],
        axis=0,
    ).astype(BF16)
    lane_hot = jnp.where(rows_of((SLOTS, rows)) == (cell_row & (SLOTS - 1)), 1.0, 0.0).astype(BF16)
    share = nt(shares, lane_hot)
    for comp in range(3):
        part = share[8 * comp : 8 * comp + 8] + share[24 + 8 * comp : 32 + 8 * comp]
        for t in range(N):
            send1[t, 2 + comp] = part

    pl.semaphore_wait(barrier, 3 * (N - 1) + 3)

    x_copies = []
    for k in FAR_FIRST:
        to = x_peer(k)
        copy = pltpu.make_async_remote_copy(
            src_ref=send1.at[to], dst_ref=recv1.at[x],
            send_sem=sx_s.at[k], recv_sem=sx_r.at[k],
            device_id={"dev": to * N + y}, device_id_type=MESH,
        )
        copy.start()
        x_copies.append(copy)
    recv1[x] = send1[x]
    for copy in x_copies:
        copy.wait_recv()
    lane_group = lanes_of((8, SLOTS)) // CAP
    for t in range(N):
        for k in range(2):
            tile = None
            for g in range(4):
                part = recv1[4 * k + g, t // 4]
                turn = (g - t % 4) % 4 * CAP
                if turn:
                    part = pltpu.roll(part, turn, 1)
                tile = part if tile is None else jnp.where(lane_group == g, part, tile)
            send2[t, k] = tile
    for comp in range(3):
        total = recv1[0, 2 + comp]
        for k in range(1, N):
            total = total + recv1[k, 2 + comp]
        for t in range(N):
            send2[t, 2 + comp] = total
    y_copies = []
    for k in FAR_FIRST:
        to = y_peer(k)
        copy = pltpu.make_async_remote_copy(
            src_ref=send2.at[to], dst_ref=recv2.at[y],
            send_sem=sy_s.at[k], recv_sem=sy_r.at[k],
            device_id={"dev": x * N + to}, device_id_type=MESH,
        )
        copy.start()
        y_copies.append(copy)
    recv2[y] = send2[y]
    for copy in y_copies:
        copy.wait_recv()
    for comp in range(3):
        total = recv2[0, 2 + comp]
        for k in range(1, N):
            total = total + recv2[k, 2 + comp]
        table_ref[core, z, comp] = total
    z_copies = []
    for k in FAR_FIRST:
        copy = pltpu.make_async_remote_copy(
            src_ref=table_ref.at[core, z], dst_ref=table_ref.at[core, z],
            send_sem=cz_s.at[k], recv_sem=cz_r.at[k],
            device_id={"grp": z_peer(k) * 2 + core}, device_id_type=MESH,
        )
        copy.start()
        z_copies.append(copy)

    slot_rows = []
    for t in range(2 * N):
        tile = recv2[t // 2, t % 2]
        spot_row = tile[4:5, :] - 1.0
        cell = jnp.floor(spot_row * (1.0 / SLOTS))
        slot = (spot_row - cell * SLOTS).astype(jnp.int32)
        cell = cell.astype(jnp.int32)
        two = split2(tile)
        slot_rows.append(jnp.where(rows_of((SLOTS, SLOTS)) == slot, 1.0, 0.0).astype(BF16))
        for c in range(CELLS):
            spread[16 * c : 16 * c + 16, t * SLOTS : (t + 1) * SLOTS] = jnp.where(
                cell == c, two, 0.0
            ).astype(BF16)
    placed = nt(spread[...], jnp.concatenate(slot_rows, axis=1))
    for c in range(CELLS):
        tile = placed[16 * c : 16 * c + 8] + placed[16 * c + 8 : 16 * c + 16]
        empty = (rows_of((8, SLOTS)) == 3) & (tile[4:5, :] == 0.0)
        ext_ref[CELLS + c] = jnp.where(empty, 1.0, tile)

    halo = []
    for i, (to, at) in enumerate(((right, 0), (left, 2 * CELLS))):
        copy = pltpu.make_async_remote_copy(
            src_ref=ext_ref.at[pl.ds(CELLS, CELLS)], dst_ref=ext_ref.at[pl.ds(at, CELLS)],
            send_sem=halo_s.at[i], recv_sem=halo_r.at[i],
            device_id={"dev": to}, device_id_type=MESH,
        )
        copy.start()
        halo.append(copy)

    for copy in z_copies:
        copy.wait_recv()
    core_copy = pltpu.make_async_remote_copy(
        src_ref=table_ref.at[core], dst_ref=table_ref.at[core],
        send_sem=cc_s.at[0], recv_sem=cc_r.at[0],
        device_id={"grp": z * 2 + (1 - core)}, device_id_type=MESH,
    )
    core_copy.start()
    for copy in [core_copy] + halo:
        copy.wait_recv()
    for copy in x_copies + y_copies + z_copies + [core_copy] + halo:
        copy.wait_send()


def halo_kernel(moved_ref, ext_ref, send_sem, recv_sem):
    dev = lax.axis_index("dev")
    right, left = (dev + 1) % (N * N), (dev + N * N - 1) % (N * N)
    barrier = pltpu.get_barrier_semaphore()
    for to in (right, left):
        pl.semaphore_signal(barrier, 1, device_id={"dev": to}, device_id_type=MESH)
    pl.semaphore_wait(barrier, 2)
    halo = []
    for i, to in enumerate((right, left)):
        copy = pltpu.make_async_remote_copy(
            src_ref=moved_ref, dst_ref=ext_ref.at[i],
            send_sem=send_sem.at[i], recv_sem=recv_sem.at[i],
            device_id={"dev": to}, device_id_type=MESH,
        )
        copy.start()
        halo.append(copy)
    for copy in halo:
        copy.wait()


def loop(count, at_once, body):
    def several(i, _):
        for u in range(at_once):
            body(i * at_once + u, 0)
        return 0

    lax.fori_loop(0, count // at_once, several, 0)


def axis_bits(ids):
    shifted = ids >> jnp.minimum(rows_of(ids.shape), 2)
    value = shifted & 1
    for bit in range(1, 5):
        value = value + ((shifted >> (3 * bit)) & 1) * (1 << bit)
    return value


def source_rows(points, half, flag):
    row = rows_of(points.shape)
    at = jnp.where(row < 3, points, 0.0)
    norm = jnp.sum(at * at, axis=0, keepdims=True) + half
    return jnp.where(row == 3, norm, jnp.where(row == 4, 1.0, jnp.where(row == 5, flag, at)))


def split3(tile):
    high = tile.astype(BF16).astype(F32)
    rest = tile - high
    mid = rest.astype(BF16).astype(F32)
    return high, mid, rest - mid


def moments(points, strength):
    sx, sy, sz = (INV_FOUR_PI * s for s in strength)
    px, py, pz = points
    row = rows_of((8, sx.shape[1]))
    tile = jnp.zeros((8, sx.shape[1]), F32)
    values = (sx, sy, sz, sy * pz - sz * py, sz * px - sx * pz, sx * py - sy * px)
    for r, value in enumerate(values):
        tile = jnp.where(row == r, value, tile)
    return split2(tile)


def pass_kernel(
    second, near_ref, own_ref, ext_ref, *rest
):
    if second:
        move_ref, moved_ref, first_ref, far_in, out_ref, feat, weight, targ, far_ids, held, halves, steps_at, acc = rest
    else:
        table_ref, far_ref, first_ref, moved_ref, far_out, feat, weight, targ, far_ids, held, halves, steps_at, acc = rest
    base_id = own_ref[0]
    base = axis_bits(jnp.full((8, SLOTS), base_id, jnp.int32))

    def put(chunk, tile):
        high, mid, low = split3(tile)
        stack = jnp.concatenate([high, high, mid, mid, high, low], axis=0)
        feat[2 * chunk] = stack.astype(BF16)
        feat[2 * chunk + 1] = pltpu.roll(stack, HALF, 1).astype(BF16)

    def put_weight(chunk, tile):
        weight[2 * chunk] = tile.astype(BF16)
        weight[2 * chunk + 1] = pltpu.roll(tile, HALF, 1).astype(BF16)

    def own_tile(l):
        tile = ext_ref[l]
        ids = jnp.full((8, SLOTS), base_id - CELLS + l, jnp.int32)
        centre = (axis_bits(ids) - base).astype(F32)
        return tile, centre

    def near_prep(l, _):
        tile, centre = own_tile(l)
        at = tile
        if second:
            side = l // CELLS
            within = l - side * CELLS
            at = jnp.where(
                side == 1, moved_ref[within],
                jnp.where(side == 0, move_ref[0, within], move_ref[1, within]),
            )
        points = at + centre
        core = tile[3:4, :]
        half = 0.5 * core * core
        put(l, source_rows(points, half, 0.0))
        put_weight(l, moments(
            (points[0:1], points[1:2], points[2:3]), (tile[5:6], tile[6:7], tile[7:8])
        ))
        filled = jnp.sum(jnp.where(tile[4:5] > 0.0, 1.0, 0.0)).astype(jnp.int32)
        held[l] = (filled + HALF - 1) >> 6

    loop(NEAR_CHUNKS, 24, near_prep)
    targ[2 * CELLS] = jnp.zeros((HALF, FEATS), BF16)
    for v in range(2):
        feat[2 * DUMMY + v] = jnp.zeros((FEATS, SLOTS), BF16)
        weight[2 * DUMMY + v] = jnp.zeros((16, SLOTS), BF16)

    def target_prep(c, _):
        tile, centre = own_tile(CELLS + c)
        at = moved_ref[c] if second else tile
        points = at + centre
        row = rows_of(points.shape)
        core = tile[3:4, :]
        half = 0.5 * core * core
        pos = jnp.where(row < 3, points, 0.0)
        norm = jnp.sum(pos * pos, axis=0, keepdims=True) + half
        value = jnp.where(
            row == 3, 1.0, jnp.where(row == 4, norm, jnp.where(row == 5, half, -2.0 * pos))
        )
        high, mid, low = split3(value)
        stack = jnp.concatenate([high, mid, high, mid, low, high], axis=0)
        stack = jnp.concatenate([stack, jnp.zeros((SLOTS - FEATS, SLOTS), F32)], axis=0)
        turned = stack.T[:, :FEATS].astype(BF16)
        targ[2 * c] = turned[:HALF]
        targ[2 * c + 1] = turned[HALF:]

    loop(CELLS, 16, target_prep)

    if not second:
        far_ids[...] = jnp.full((CELLS, 2 * SLOTS), -1, jnp.int32)
        far_ids[:, 0:FAR] = far_ref[...]
        table = table_ref[...].reshape(2 * N * 3 * N, SLOTS)
        table_high = table.astype(BF16)
        table_low = (table - table_high.astype(F32)).astype(BF16)
        table2 = jnp.concatenate([table_high, table_low], axis=1)

        def far_gather(c, _):
            ids = far_ids[pl.ds(c, 1), :]
            lane_hot = jnp.where(rows_of((SLOTS, 256)) == (ids & 127), 1.0, 0.0).astype(BF16)
            got = nn(table2, jnp.concatenate([lane_hot, lane_hot], axis=0))
            high = ids >> 7
            sums = [jnp.zeros((8, 256), F32) for _ in range(3)]
            for g in range(2 * N):
                start = (g % 2) * N * 3 * N + (g // 2) * 3 * N
                here = rows_of((8, 256)) + g * N == high
                for comp in range(3):
                    part = got[start + comp * N : start + comp * N + N]
                    sums[comp] = sums[comp] + jnp.where(here, part, 0.0)
            strength = [jnp.sum(s, axis=0, keepdims=True) for s in sums]
            spots = axis_bits(jnp.broadcast_to(jnp.maximum(ids, 0), (8, 256)))
            points = (spots - jnp.concatenate([base, base], axis=1)).astype(F32)
            row = rows_of(points.shape)
            tile = jnp.where(row < 3, points, 0.0)
            for comp in range(3):
                tile = jnp.where(row == 5 + comp, strength[comp], tile)
            far_out[2 * c] = tile[:, :SLOTS]
            far_out[2 * c + 1] = tile[:, SLOTS:]

        loop(CELLS, 4, far_gather)
        far = far_out
    else:
        far = far_in

    def far_prep(i, _):
        tile = far[i]
        put(FAR_BASE + i, source_rows(tile, 0.0, 1.0))
        put_weight(FAR_BASE + i, moments(
            (tile[0:1], tile[1:2], tile[2:3]), (tile[5:6], tile[6:7], tile[7:8])
        ))

    loop(2 * CELLS, 32, far_prep)

    first_near = base_id - CELLS

    def listing(c, total):
        start = c * LIST
        for i in range(3):
            halves[start + i] = 2 * FAR_BASE + 4 * c + i
        n = start + 3
        for e in range(NEAR):
            near = near_ref[e, c]
            at = jnp.where(near >= 0, near - first_near, DUMMY)
            halves[n] = 2 * at
            halves[n + 1] = 2 * at + 1
            n = n + held[at]
        for i in range(3):
            halves[n + i] = 2 * DUMMY
        rounds = (n - start + 3) >> 2
        size = held[CELLS + c]
        for h in range(2):
            for j in range(8):
                steps_at[total + j] = (start + 4 * j) * 64 + 2 * c + h
            total = total + jnp.where(size > h, rounds, 0)
        return total

    held[DUMMY] = 0
    total = lax.fori_loop(0, CELLS, listing, jnp.int32(0))
    for i in range(4):
        halves[CELLS * LIST + i] = 2 * DUMMY
    for p in range(UNROLL):
        steps_at[total + p] = CELLS * LIST * 64 + 2 * CELLS
    acc[...] = jnp.zeros(acc.shape, F32)

    def joined(ref, rows, four):
        low = lanes_of((rows, SLOTS)) < HALF
        return jnp.concatenate(
            [jnp.where(low, ref[four[i]], ref[four[i + 1] ^ 1]) for i in (0, 2)], axis=1
        )

    def powers(dist):
        root = lax.rsqrt(jnp.maximum(dist, 0.08))
        q = root * root * root
        q_high = q.astype(BF16)
        return q_high, (q - q_high.astype(F32)).astype(BF16)

    def steps(i, _):
        words = [steps_at[i * UNROLL + u] for u in range(UNROLL)]
        targets = [word & 63 for word in words]
        starts = [word >> 6 for word in words]
        fours = [[halves[p + j] for j in range(4)] for p in starts]
        dists = [nn(targ[t], joined(feat, FEATS, f)) for t, f in zip(targets, fours)]
        qs = [powers(d) for d in dists]
        parts = []
        for (high, low), f in zip(qs, fours):
            w = joined(weight, 16, f)
            parts.append(nt(high, w) + nt(low, w))
        for t, part in zip(targets, parts):
            acc[t] += part
        return 0

    lax.fori_loop(0, (total + UNROLL - 1) // UNROLL, steps, 0)

    def cell(c, _):
        full = jnp.concatenate([acc[2 * c], acc[2 * c + 1]], axis=0)
        full = jnp.concatenate([full, jnp.zeros((SLOTS, SLOTS - 16), F32)], axis=1).T
        sums = full[0:8] + full[8:16]
        tile, centre = own_tile(CELLS + c)
        at = moved_ref[c] if second else tile
        points = at + centre
        px, py, pz = points[0:1], points[1:2], points[2:3]
        bx, by, bz, ax, ay, az = (sums[r : r + 1] for r in range(6))
        row = rows_of((8, SLOTS))
        vel = jnp.where(
            row == 0, by * pz - bz * py - ax,
            jnp.where(row == 1, bz * px - bx * pz - ay, bx * py - by * px - az),
        )
        vel = jnp.where((row < 3) & (tile[4:5] > 0.0), vel, 0.0)
        if second:
            mean = 0.5 * (first_ref[c] + vel)
            out_ref[:, pl.ds(pl.multiple_of(c * SLOTS, SLOTS), SLOTS)] = mean[0:3]
        else:
            first_ref[c] = vel
            moved_ref[c] = jnp.where(row < 3, tile + 0.25 * vel, 0.0)

    loop(CELLS, 16, cell)


def run_pass(second, near_list, own_base, ext, *more):
    vmem = pl.BlockSpec(memory_space=pltpu.VMEM)
    smem = pl.BlockSpec(memory_space=pltpu.SMEM)
    tiles = jax.ShapeDtypeStruct((CELLS, 8, SLOTS), F32)
    flat = jax.ShapeDtypeStruct((3, CELLS * SLOTS), F32)
    outs = flat if second else (tiles, tiles, jax.ShapeDtypeStruct((2 * CELLS, 8, SLOTS), F32))
    return pl.pallas_call(
        functools.partial(pass_kernel, second),
        out_shape=outs,
        in_specs=[smem, smem, vmem] + [vmem] * len(more),
        out_specs=vmem if second else (vmem,) * 3,
        scratch_shapes=[
            pltpu.VMEM((2 * CHUNKS, FEATS, SLOTS), BF16),
            pltpu.VMEM((2 * CHUNKS, 16, SLOTS), BF16),
            pltpu.VMEM((2 * CELLS + 1, HALF, FEATS), BF16),
            pltpu.VMEM((CELLS, 2 * SLOTS), jnp.int32),
            pltpu.SMEM((NEAR_CHUNKS + 1,), jnp.int32),
            pltpu.SMEM((CELLS * LIST + 4,), jnp.int32),
            pltpu.SMEM((CELLS * 16 + 8 + UNROLL,), jnp.int32),
            pltpu.VMEM((2 * CELLS + 1, HALF, 16), F32),
        ],
        compiler_params=pltpu.CompilerParams(vmem_limit_bytes=40 * 1024 * 1024),
    )(near_list, own_base, ext, *more)


def route(offsets, strengths, cores, place):
    spots = place[0:1] * SLOTS + place[1:2]
    tile_rows = jnp.concatenate(
        [offsets, cores.reshape(1, -1), spots.astype(F32), strengths], axis=0
    )
    vmem = pl.BlockSpec(memory_space=pltpu.VMEM)
    sems = [pltpu.SemaphoreType.DMA((N,))] * 6 + [pltpu.SemaphoreType.DMA((2,))] * 4
    return pl.pallas_call(
        route_kernel,
        out_shape=(
            jax.ShapeDtypeStruct((3 * CELLS, 8, SLOTS), F32),
            jax.ShapeDtypeStruct((2, N, 3, N, SLOTS), F32),
        ),
        in_specs=[vmem],
        out_specs=(vmem, vmem),
        scratch_shapes=[
            pltpu.VMEM((8, offsets.shape[1]), F32),
            pltpu.VMEM((256, 2 * N * SLOTS), BF16),
            pltpu.VMEM((N, 5, 8, SLOTS), F32),
            pltpu.VMEM((N, 5, 8, SLOTS), F32),
            pltpu.VMEM((N, 5, 8, SLOTS), F32),
            pltpu.VMEM((N, 5, 8, SLOTS), F32),
        ] + sems,
        compiler_params=pltpu.CompilerParams(
            collective_id=0, has_side_effects=True, vmem_limit_bytes=40 * 1024 * 1024
        ),
    )(tile_rows)


def exchange(moved):
    vmem = pl.BlockSpec(memory_space=pltpu.VMEM)
    return pl.pallas_call(
        halo_kernel,
        out_shape=jax.ShapeDtypeStruct((2, CELLS, 8, SLOTS), F32),
        in_specs=[vmem],
        out_specs=vmem,
        scratch_shapes=[pltpu.SemaphoreType.DMA((2,)), pltpu.SemaphoreType.DMA((2,))],
        compiler_params=pltpu.CompilerParams(
            collective_id=1, has_side_effects=True, vmem_limit_bytes=8 * 1024 * 1024
        ),
    )(moved)


def per_device(offsets, strengths, cores, place, near_list, far_list):
    device = lax.axis_index("grp") * (N * N) + lax.axis_index("dev")
    own_base = (device * CELLS).astype(jnp.int32).reshape(1)
    ext, table = route(offsets, strengths, cores, place)
    first, moved, far = run_pass(False, near_list, own_base, ext, table, far_list.T)
    move = exchange(moved)
    return run_pass(True, near_list, own_base, ext, move, moved, first, far)


def solution(mesh):
    row = P(None, ("grp", "dev"))
    return jax.shard_map(
        per_device, mesh=mesh, in_specs=(row, row, P(("grp", "dev")), row, row, row),
        out_specs=row, check_vma=False,
    )
```

```python
import functools
import math

import jax
import jax.numpy as jnp
from jax import lax
from jax.experimental import pallas as pl
from jax.experimental.pallas import tpu as pltpu
from jax.sharding import PartitionSpec as P

SLOTS = 128
CELLS = 16
CAP = 32
NEAR = 14
FAR = 189
N = 8
INV_FOUR_PI = 0.25 / math.pi
MESH = pl.DeviceIdType.MESH
F32 = jnp.float32
BF16 = jnp.bfloat16

NEAR_CHUNKS = 3 * CELLS
DUMMY = NEAR_CHUNKS
FAR_BASE = NEAR_CHUNKS + 2
CHUNKS = FAR_BASE + 2 * CELLS
FEATS = 48
HALF = SLOTS // 2
LIST = 40
UNROLL = 12
LAST = CELLS * 16 + 8 + UNROLL
FAR_FIRST = (4, 3, 5, 2, 6, 1, 7)


def nt(a, b):
    return lax.dot_general(a, b, (((1,), (1,)), ((), ())), preferred_element_type=F32)


def nn(a, b):
    return lax.dot_general(a, b, (((1,), (0,)), ((), ())), preferred_element_type=F32)


def rows_of(shape):
    return lax.broadcasted_iota(jnp.int32, shape, len(shape) - 2)


def lanes_of(shape):
    return lax.broadcasted_iota(jnp.int32, shape, len(shape) - 1)


def split2(value):
    high = value.astype(BF16).astype(F32)
    return jnp.concatenate([high, value - high], axis=0)


def route_kernel(
    rows_ref, ext_ref, table_ref, fields, spread, send1, recv1, send2, recv2,
    sx_s, sx_r, sy_s, sy_r, cz_s, cz_r, halo_s, halo_r, cc_s, cc_r,
):
    dev = lax.axis_index("dev")
    grp = lax.axis_index("grp")
    x, y = dev // N, dev % N
    z, core = grp // 2, grp % 2

    def x_peer(k):
        return (x + k) % N

    def y_peer(k):
        return (y + k) % N

    def z_peer(k):
        return (z + k) % N

    right, left = (dev + 1) % (N * N), (dev + N * N - 1) % (N * N)
    barrier = pltpu.get_barrier_semaphore()
    for k in range(1, N):
        pl.semaphore_signal(barrier, 1, device_id={"dev": x_peer(k) * N + y}, device_id_type=MESH)
        pl.semaphore_signal(barrier, 1, device_id={"dev": x * N + y_peer(k)}, device_id_type=MESH)
        pl.semaphore_signal(barrier, 1, device_id={"grp": z_peer(k) * 2 + core}, device_id_type=MESH)
    pl.semaphore_signal(barrier, 1, device_id={"dev": right}, device_id_type=MESH)
    pl.semaphore_signal(barrier, 1, device_id={"dev": left}, device_id_type=MESH)
    pl.semaphore_signal(barrier, 1, device_id={"grp": z * 2 + (1 - core)}, device_id_type=MESH)

    rows = rows_ref.shape[1]
    place = rows_ref[4:5, :].astype(jnp.int32)
    cell_row = place >> 7
    spot = (place & (CELLS * SLOTS - 1)) + 1
    owner = (cell_row >> 4) & (N * N - 1)
    fields[...] = jnp.where(rows_of((8, rows)) == 4, spot.astype(F32), rows_ref[...])
    both = split2(fields[...])
    earlier = rows_of((SLOTS, 2 * SLOTS)) < lanes_of((SLOTS, 2 * SLOTS))
    counter = jnp.where(earlier | (lanes_of((SLOTS, 2 * SLOTS)) >= SLOTS), 1.0, 0.0).astype(BF16)
    carry = jnp.zeros((N * N, SLOTS), F32)
    ranks = []
    for b in range(rows // SLOTS):
        hot = jnp.where(rows_of((N * N, SLOTS)) == owner[:, b * SLOTS : (b + 1) * SLOTS], 1.0, 0.0)
        count = nn(hot.astype(BF16), counter)
        ranks.append(jnp.sum(hot * (count[:, :SLOTS] + carry), axis=0, keepdims=True))
        carry = carry + count[:, SLOTS:]
    rank = jnp.concatenate(ranks, axis=1).astype(jnp.int32)
    low = (owner & 3) * CAP + rank
    high = owner >> 2
    low_hot = jnp.where(rows_of((SLOTS, rows)) == low, 1.0, 0.0).astype(BF16)
    for t in range(2 * N):
        spread[16 * t : 16 * t + 16, 0:rows] = jnp.where(high == t, both, 0.0).astype(BF16)
    packed = nt(spread[:, 0:rows], low_hot)
    for t in range(2 * N):
        send1[t // 2, t % 2] = packed[16 * t : 16 * t + 8] + packed[16 * t + 8 : 16 * t + 16]

    owner_x = owner >> 3
    shares = jnp.concatenate(
        [jnp.where(rows_of((8, rows)) == owner_x, both[r : r + 1], 0.0) for r in (5, 6, 7, 13, 14, 15)],
        axis=0,
    ).astype(BF16)
    lane_hot = jnp.where(rows_of((SLOTS, rows)) == (cell_row & (SLOTS - 1)), 1.0, 0.0).astype(BF16)
    share = nt(shares, lane_hot)
    for comp in range(3):
        part = share[8 * comp : 8 * comp + 8] + share[24 + 8 * comp : 32 + 8 * comp]
        for t in range(N):
            send1[t, 2 + comp] = part

    pl.semaphore_wait(barrier, 3 * (N - 1) + 3)

    x_copies = []
    for k in FAR_FIRST:
        to = x_peer(k)
        copy = pltpu.make_async_remote_copy(
            src_ref=send1.at[to], dst_ref=recv1.at[x],
            send_sem=sx_s.at[k], recv_sem=sx_r.at[k],
            device_id={"dev": to * N + y}, device_id_type=MESH,
        )
        copy.start()
        x_copies.append(copy)
    recv1[x] = send1[x]
    for copy in x_copies:
        copy.wait_recv()
    lane_group = lanes_of((8, SLOTS)) // CAP
    for t in range(N):
        for k in range(2):
            tile = None
            for g in range(4):
                part = recv1[4 * k + g, t // 4]
                turn = (g - t % 4) % 4 * CAP
                if turn:
                    part = pltpu.roll(part, turn, 1)
                tile = part if tile is None else jnp.where(lane_group == g, part, tile)
            send2[t, k] = tile
    for comp in range(3):
        total = recv1[0, 2 + comp]
        for k in range(1, N):
            total = total + recv1[k, 2 + comp]
        for t in range(N):
            send2[t, 2 + comp] = total
    y_copies = []
    for k in FAR_FIRST:
        to = y_peer(k)
        copy = pltpu.make_async_remote_copy(
            src_ref=send2.at[to], dst_ref=recv2.at[y],
            send_sem=sy_s.at[k], recv_sem=sy_r.at[k],
            device_id={"dev": x * N + to}, device_id_type=MESH,
        )
        copy.start()
        y_copies.append(copy)
    recv2[y] = send2[y]
    for copy in y_copies:
        copy.wait_recv()
    for comp in range(3):
        total = recv2[0, 2 + comp]
        for k in range(1, N):
            total = total + recv2[k, 2 + comp]
        table_ref[core, z, comp] = total
    z_copies = []
    for k in FAR_FIRST:
        copy = pltpu.make_async_remote_copy(
            src_ref=table_ref.at[core, z], dst_ref=table_ref.at[core, z],
            send_sem=cz_s.at[k], recv_sem=cz_r.at[k],
            device_id={"grp": z_peer(k) * 2 + core}, device_id_type=MESH,
        )
        copy.start()
        z_copies.append(copy)

    slot_rows = []
    for t in range(2 * N):
        tile = recv2[t // 2, t % 2]
        spot_row = tile[4:5, :] - 1.0
        cell = jnp.floor(spot_row * (1.0 / SLOTS))
        slot = (spot_row - cell * SLOTS).astype(jnp.int32)
        cell = cell.astype(jnp.int32)
        two = split2(tile)
        slot_rows.append(jnp.where(rows_of((SLOTS, SLOTS)) == slot, 1.0, 0.0).astype(BF16))
        for c in range(CELLS):
            spread[16 * c : 16 * c + 16, t * SLOTS : (t + 1) * SLOTS] = jnp.where(
                cell == c, two, 0.0
            ).astype(BF16)
    placed = nt(spread[...], jnp.concatenate(slot_rows, axis=1))
    for c in range(CELLS):
        tile = placed[16 * c : 16 * c + 8] + placed[16 * c + 8 : 16 * c + 16]
        empty = (rows_of((8, SLOTS)) == 3) & (tile[4:5, :] == 0.0)
        ext_ref[CELLS + c] = jnp.where(empty, 1.0, tile)

    halo = []
    for i, (to, at) in enumerate(((right, 0), (left, 2 * CELLS))):
        copy = pltpu.make_async_remote_copy(
            src_ref=ext_ref.at[pl.ds(CELLS, CELLS)], dst_ref=ext_ref.at[pl.ds(at, CELLS)],
            send_sem=halo_s.at[i], recv_sem=halo_r.at[i],
            device_id={"dev": to}, device_id_type=MESH,
        )
        copy.start()
        halo.append(copy)

    for copy in z_copies:
        copy.wait_recv()
    core_copy = pltpu.make_async_remote_copy(
        src_ref=table_ref.at[core], dst_ref=table_ref.at[core],
        send_sem=cc_s.at[0], recv_sem=cc_r.at[0],
        device_id={"grp": z * 2 + (1 - core)}, device_id_type=MESH,
    )
    core_copy.start()
    for copy in [core_copy] + halo:
        copy.wait_recv()
    for copy in x_copies + y_copies + z_copies + [core_copy] + halo:
        copy.wait_send()


def halo_kernel(moved_ref, ext_ref, send_sem, recv_sem):
    dev = lax.axis_index("dev")
    right, left = (dev + 1) % (N * N), (dev + N * N - 1) % (N * N)
    barrier = pltpu.get_barrier_semaphore()
    for to in (right, left):
        pl.semaphore_signal(barrier, 1, device_id={"dev": to}, device_id_type=MESH)
    pl.semaphore_wait(barrier, 2)
    halo = []
    for i, to in enumerate((right, left)):
        copy = pltpu.make_async_remote_copy(
            src_ref=moved_ref, dst_ref=ext_ref.at[i],
            send_sem=send_sem.at[i], recv_sem=recv_sem.at[i],
            device_id={"dev": to}, device_id_type=MESH,
        )
        copy.start()
        halo.append(copy)
    for copy in halo:
        copy.wait()


def loop(count, at_once, body):
    def several(i, _):
        for u in range(at_once):
            body(i * at_once + u, 0)
        return 0

    lax.fori_loop(0, count // at_once, several, 0)


def axis_bits(ids):
    shifted = ids >> jnp.minimum(rows_of(ids.shape), 2)
    value = shifted & 1
    for bit in range(1, 5):
        value = value + ((shifted >> (3 * bit)) & 1) * (1 << bit)
    return value


def source_rows(points, half, flag):
    row = rows_of(points.shape)
    at = jnp.where(row < 3, points, 0.0)
    norm = jnp.sum(at * at, axis=0, keepdims=True) + half
    return jnp.where(row == 3, norm, jnp.where(row == 4, 1.0, jnp.where(row == 5, flag, at)))


def split3(tile):
    high = tile.astype(BF16).astype(F32)
    rest = tile - high
    mid = rest.astype(BF16).astype(F32)
    return high, mid, rest - mid


def moments(points, strength):
    sx, sy, sz = (INV_FOUR_PI * s for s in strength)
    px, py, pz = points
    row = rows_of((8, sx.shape[1]))
    tile = jnp.zeros((8, sx.shape[1]), F32)
    values = (sx, sy, sz, sy * pz - sz * py, sz * px - sx * pz, sx * py - sy * px)
    for r, value in enumerate(values):
        tile = jnp.where(row == r, value, tile)
    return split2(tile)


def pass_kernel(
    second, near_ref, own_ref, ext_ref, *rest
):
    if second:
        move_ref, moved_ref, first_ref, far_in, halves, steps_at, out_ref, feat, weight, targ, acc = rest
    else:
        table_ref, far_ref, first_ref, moved_ref, far_out, halves, steps_at, feat, weight, targ, acc, far_ids, held = rest
    base_id = own_ref[0]
    base = axis_bits(jnp.full((8, SLOTS), base_id, jnp.int32))

    def put(chunk, tile):
        high, mid, low = split3(tile)
        stack = jnp.concatenate([high, high, mid, mid, high, low], axis=0)
        feat[2 * chunk] = stack.astype(BF16)
        feat[2 * chunk + 1] = pltpu.roll(stack, HALF, 1).astype(BF16)

    def put_weight(chunk, tile):
        weight[2 * chunk] = tile.astype(BF16)
        weight[2 * chunk + 1] = pltpu.roll(tile, HALF, 1).astype(BF16)

    def own_tile(l):
        tile = ext_ref[l]
        ids = jnp.full((8, SLOTS), base_id - CELLS + l, jnp.int32)
        centre = (axis_bits(ids) - base).astype(F32)
        return tile, centre

    def near_prep(l, _):
        tile, centre = own_tile(l)
        at = tile
        if second:
            side = l // CELLS
            within = l - side * CELLS
            at = jnp.where(
                side == 1, moved_ref[within],
                jnp.where(side == 0, move_ref[0, within], move_ref[1, within]),
            )
        points = at + centre
        core = tile[3:4, :]
        half = 0.5 * core * core
        put(l, source_rows(points, half, 0.0))
        put_weight(l, moments(
            (points[0:1], points[1:2], points[2:3]), (tile[5:6], tile[6:7], tile[7:8])
        ))
        if not second:
            filled = jnp.sum(jnp.where(tile[4:5] > 0.0, 1.0, 0.0)).astype(jnp.int32)
            held[l] = (filled + HALF - 1) >> 6

    loop(NEAR_CHUNKS, 24, near_prep)
    targ[2 * CELLS] = jnp.zeros((HALF, FEATS), BF16)
    for v in range(2):
        feat[2 * DUMMY + v] = jnp.zeros((FEATS, SLOTS), BF16)
        weight[2 * DUMMY + v] = jnp.zeros((16, SLOTS), BF16)

    def target_prep(c, _):
        tile, centre = own_tile(CELLS + c)
        at = moved_ref[c] if second else tile
        points = at + centre
        row = rows_of(points.shape)
        core = tile[3:4, :]
        half = 0.5 * core * core
        pos = jnp.where(row < 3, points, 0.0)
        norm = jnp.sum(pos * pos, axis=0, keepdims=True) + half
        value = jnp.where(
            row == 3, 1.0, jnp.where(row == 4, norm, jnp.where(row == 5, half, -2.0 * pos))
        )
        high, mid, low = split3(value)
        stack = jnp.concatenate([high, mid, high, mid, low, high], axis=0)
        stack = jnp.concatenate([stack, jnp.zeros((SLOTS - FEATS, SLOTS), F32)], axis=0)
        turned = stack.T[:, :FEATS].astype(BF16)
        targ[2 * c] = turned[:HALF]
        targ[2 * c + 1] = turned[HALF:]

    loop(CELLS, 16, target_prep)

    if not second:
        far_ids[...] = jnp.full((CELLS, 2 * SLOTS), -1, jnp.int32)
        far_ids[:, 0:FAR] = far_ref[...]
        table = table_ref[...].reshape(2 * N * 3 * N, SLOTS)
        table_high = table.astype(BF16)
        table_low = (table - table_high.astype(F32)).astype(BF16)
        table2 = jnp.concatenate([table_high, table_low], axis=1)

        def far_gather(c, _):
            ids = far_ids[pl.ds(c, 1), :]
            lane_hot = jnp.where(rows_of((SLOTS, 256)) == (ids & 127), 1.0, 0.0).astype(BF16)
            got = nn(table2, jnp.concatenate([lane_hot, lane_hot], axis=0))
            high = ids >> 7
            sums = [jnp.zeros((8, 256), F32) for _ in range(3)]
            for g in range(2 * N):
                start = (g % 2) * N * 3 * N + (g // 2) * 3 * N
                here = rows_of((8, 256)) + g * N == high
                for comp in range(3):
                    part = got[start + comp * N : start + comp * N + N]
                    sums[comp] = sums[comp] + jnp.where(here, part, 0.0)
            strength = [jnp.sum(s, axis=0, keepdims=True) for s in sums]
            spots = axis_bits(jnp.broadcast_to(jnp.maximum(ids, 0), (8, 256)))
            points = (spots - jnp.concatenate([base, base], axis=1)).astype(F32)
            row = rows_of(points.shape)
            tile = jnp.where(row < 3, points, 0.0)
            for comp in range(3):
                tile = jnp.where(row == 5 + comp, strength[comp], tile)
            far_out[2 * c] = tile[:, :SLOTS]
            far_out[2 * c + 1] = tile[:, SLOTS:]

        loop(CELLS, 4, far_gather)
        far = far_out
    else:
        far = far_in

    def far_prep(i, _):
        tile = far[i]
        put(FAR_BASE + i, source_rows(tile, 0.0, 1.0))
        put_weight(FAR_BASE + i, moments(
            (tile[0:1], tile[1:2], tile[2:3]), (tile[5:6], tile[6:7], tile[7:8])
        ))

    loop(2 * CELLS, 32, far_prep)

    first_near = base_id - CELLS

    def listing(c, total):
        start = c * LIST
        for i in range(3):
            halves[start + i] = 2 * FAR_BASE + 4 * c + i
        n = start + 3
        for e in range(NEAR):
            near = near_ref[e, c]
            at = jnp.where(near >= 0, near - first_near, DUMMY)
            halves[n] = 2 * at
            halves[n + 1] = 2 * at + 1
            n = n + held[at]
        for i in range(3):
            halves[n + i] = 2 * DUMMY
        rounds = (n - start + 3) >> 2
        size = held[CELLS + c]
        for h in range(2):
            for j in range(8):
                steps_at[total + j] = (start + 4 * j) * 64 + 2 * c + h
            total = total + jnp.where(size > h, rounds, 0)
        return total

    if second:
        total = steps_at[LAST]
    else:
        held[DUMMY] = 0
        total = lax.fori_loop(0, CELLS, listing, jnp.int32(0))
        for i in range(4):
            halves[CELLS * LIST + i] = 2 * DUMMY
        for p in range(UNROLL):
            steps_at[total + p] = CELLS * LIST * 64 + 2 * CELLS
        steps_at[LAST] = total
    acc[...] = jnp.zeros(acc.shape, F32)

    def joined(ref, rows, four):
        low = lanes_of((rows, SLOTS)) < HALF
        return jnp.concatenate(
            [jnp.where(low, ref[four[i]], ref[four[i + 1] ^ 1]) for i in (0, 2)], axis=1
        )

    def powers(dist):
        root = lax.rsqrt(jnp.maximum(dist, 0.08))
        q = root * root * root
        q_high = q.astype(BF16)
        return q_high, (q - q_high.astype(F32)).astype(BF16)

    def steps(i, _):
        words = [steps_at[i * UNROLL + u] for u in range(UNROLL)]
        targets = [word & 63 for word in words]
        starts = [word >> 6 for word in words]
        fours = [[halves[p + j] for j in range(4)] for p in starts]
        dists = [nn(targ[t], joined(feat, FEATS, f)) for t, f in zip(targets, fours)]
        qs = [powers(d) for d in dists]
        parts = []
        for (high, low), f in zip(qs, fours):
            w = joined(weight, 16, f)
            parts.append(nt(high, w) + nt(low, w))
        for t, part in zip(targets, parts):
            acc[t] += part
        return 0

    lax.fori_loop(0, (total + UNROLL - 1) // UNROLL, steps, 0)

    def cell(c, _):
        full = jnp.concatenate([acc[2 * c], acc[2 * c + 1]], axis=0)
        full = jnp.concatenate([full, jnp.zeros((SLOTS, SLOTS - 16), F32)], axis=1).T
        sums = full[0:8] + full[8:16]
        tile, centre = own_tile(CELLS + c)
        at = moved_ref[c] if second else tile
        points = at + centre
        px, py, pz = points[0:1], points[1:2], points[2:3]
        bx, by, bz, ax, ay, az = (sums[r : r + 1] for r in range(6))
        row = rows_of((8, SLOTS))
        vel = jnp.where(
            row == 0, by * pz - bz * py - ax,
            jnp.where(row == 1, bz * px - bx * pz - ay, bx * py - by * px - az),
        )
        vel = jnp.where((row < 3) & (tile[4:5] > 0.0), vel, 0.0)
        if second:
            mean = 0.5 * (first_ref[c] + vel)
            out_ref[:, pl.ds(pl.multiple_of(c * SLOTS, SLOTS), SLOTS)] = mean[0:3]
        else:
            first_ref[c] = vel
            moved_ref[c] = jnp.where(row < 3, tile + 0.25 * vel, 0.0)

    loop(CELLS, 16, cell)


def run_pass(second, near_list, own_base, ext, *more):
    vmem = pl.BlockSpec(memory_space=pltpu.VMEM)
    smem = pl.BlockSpec(memory_space=pltpu.SMEM)
    tiles = jax.ShapeDtypeStruct((CELLS, 8, SLOTS), F32)
    flat = jax.ShapeDtypeStruct((3, CELLS * SLOTS), F32)
    lists = (
        jax.ShapeDtypeStruct((CELLS * LIST + 4,), jnp.int32),
        jax.ShapeDtypeStruct((LAST + 1,), jnp.int32),
    )
    far = jax.ShapeDtypeStruct((2 * CELLS, 8, SLOTS), F32)
    outs = flat if second else (tiles, tiles, far) + lists
    ins = [vmem] * (len(more) - 2) + [smem] * 2 if second else [vmem] * len(more)
    extra = [] if second else [
        pltpu.VMEM((CELLS, 2 * SLOTS), jnp.int32), pltpu.SMEM((NEAR_CHUNKS + 1,), jnp.int32)
    ]
    return pl.pallas_call(
        functools.partial(pass_kernel, second),
        out_shape=outs,
        in_specs=[smem, smem, vmem] + ins,
        out_specs=vmem if second else (vmem,) * 3 + (smem,) * 2,
        scratch_shapes=[
            pltpu.VMEM((2 * CHUNKS, FEATS, SLOTS), BF16),
            pltpu.VMEM((2 * CHUNKS, 16, SLOTS), BF16),
            pltpu.VMEM((2 * CELLS + 1, HALF, FEATS), BF16),
            pltpu.VMEM((2 * CELLS + 1, HALF, 16), F32),
        ] + extra,
        compiler_params=pltpu.CompilerParams(vmem_limit_bytes=40 * 1024 * 1024),
    )(near_list, own_base, ext, *more)


def route(offsets, strengths, cores, place):
    spots = place[0:1] * SLOTS + place[1:2]
    tile_rows = jnp.concatenate(
        [offsets, cores.reshape(1, -1), spots.astype(F32), strengths], axis=0
    )
    vmem = pl.BlockSpec(memory_space=pltpu.VMEM)
    sems = [pltpu.SemaphoreType.DMA((N,))] * 6 + [pltpu.SemaphoreType.DMA((2,))] * 4
    return pl.pallas_call(
        route_kernel,
        out_shape=(
            jax.ShapeDtypeStruct((3 * CELLS, 8, SLOTS), F32),
            jax.ShapeDtypeStruct((2, N, 3, N, SLOTS), F32),
        ),
        in_specs=[vmem],
        out_specs=(vmem, vmem),
        scratch_shapes=[
            pltpu.VMEM((8, offsets.shape[1]), F32),
            pltpu.VMEM((256, 2 * N * SLOTS), BF16),
            pltpu.VMEM((N, 5, 8, SLOTS), F32),
            pltpu.VMEM((N, 5, 8, SLOTS), F32),
            pltpu.VMEM((N, 5, 8, SLOTS), F32),
            pltpu.VMEM((N, 5, 8, SLOTS), F32),
        ] + sems,
        compiler_params=pltpu.CompilerParams(
            collective_id=0, has_side_effects=True, vmem_limit_bytes=40 * 1024 * 1024
        ),
    )(tile_rows)


def exchange(moved):
    vmem = pl.BlockSpec(memory_space=pltpu.VMEM)
    return pl.pallas_call(
        halo_kernel,
        out_shape=jax.ShapeDtypeStruct((2, CELLS, 8, SLOTS), F32),
        in_specs=[vmem],
        out_specs=vmem,
        scratch_shapes=[pltpu.SemaphoreType.DMA((2,)), pltpu.SemaphoreType.DMA((2,))],
        compiler_params=pltpu.CompilerParams(
            collective_id=1, has_side_effects=True, vmem_limit_bytes=8 * 1024 * 1024
        ),
    )(moved)


def per_device(offsets, strengths, cores, place, near_list, far_list):
    device = lax.axis_index("grp") * (N * N) + lax.axis_index("dev")
    own_base = (device * CELLS).astype(jnp.int32).reshape(1)
    ext, table = route(offsets, strengths, cores, place)
    first, moved, far, halves, steps_at = run_pass(False, near_list, own_base, ext, table, far_list.T)
    move = exchange(moved)
    return run_pass(True, near_list, own_base, ext, move, moved, first, far, halves, steps_at)


def solution(mesh):
    row = P(None, ("grp", "dev"))
    return jax.shard_map(
        per_device, mesh=mesh, in_specs=(row, row, P(("grp", "dev")), row, row, row),
        out_specs=row, check_vma=False,
    )
```
